128 devices in a mesh: seq: 16 (over z, y), tp: 8 (over x, core).
Axes of the slice: x: 4, y: 4, z: 4, core: 2. Of those that a mesh axis runs over, the one named last changes fastest.
Arguments:
- tokens: bfloat16 [8192, 4096], P('seq'), may hold values from -6 to 6
- norm_gain: float32 [4096], replicated, may hold values from 0.1 to 1.9
- w_query: bfloat16 [4096, 4096], P(None, 'tp'), may hold values from -2.5 to 2.5
- w_key: bfloat16 [4096, 1024], P(None, 'tp'), may hold values from -0.09375 to 0.09375
- w_value: bfloat16 [4096, 1024], P(None, 'tp'), may hold values from -0.09375 to 0.09375
- w_out: bfloat16 [4096, 4096], P('tp'), may hold values from -0.75 to 0.75
- doc_ids: int32 [64], replicated, may hold values from 0 to 7, never falling along the last dimension, each value on 1 to 36 neighbouring positions
Outputs:
- attended: bfloat16 [8192, 4096], P(('seq', 'tp'))
The draws below stay inside these ranges and needn't reach their ends.
Inputs may be any that keep to these rules, and one draw needn't show every extreme that they name: `doc_ids`: never decreasing; each document covers 1 to 36 blocks and one covers exactly 36.
All inputs are finite; a program needn't handle non-finite values.
Results may differ from the reference program's by a relative error of at most 0.019.
Values may be sent and summed in bfloat16 or wider, within the bound.
A program may use at most 64 MiB of HBM per device.

```python
import math
import jax
import jax.numpy as jnp
import numpy as np
from jax import lax

D = 4096
H = 32
KVH = 8
HD = 128
BLK = 128
TOKENS = 8192
NB = 64
DOCS = 8
MAXDOC = 36
N_TP = 8


def shared_columns(key):
    shared_key = jax.random.fold_in(key, 3)
    return jnp.clip(jax.random.normal(shared_key, (D, KVH * HD), jnp.float32), -6.0, 6.0) * D ** (-0.5)


def draw_w_key(key, part):
    columns = shared_columns(key)
    return jnp.clip(columns, -0.09375, 0.09375).astype(jnp.bfloat16)


def draw_w_query(key, part):
    key = jax.random.fold_in(key, 7)
    random_key = jax.random.fold_in(key, 0)
    random_part = jnp.clip(jax.random.normal(random_key, (D, H * HD), jnp.float32), -6.0, 6.0) * D ** (-0.5)
    return jnp.clip(random_part, -2.5, 2.5).astype(jnp.bfloat16)


def level_of(key, extent, cuts, low, top_value):
    def one(axis_at, parts):
        heights = jax.random.uniform(jax.random.fold_in(jax.random.fold_in(key, 6), axis_at), (parts,), jnp.float32, low / len(cuts), top_value / len(cuts))
        return jnp.repeat(jnp.exp(heights), extent[axis_at] // parts).reshape((-1,) + (1,) * (len(extent) - axis_at - 1))

    factor_of = one(*cuts[0])
    for cut in cuts[1:]:
        factor_of = factor_of * one(*cut)
    return factor_of


def profile(count, total, most, lean):
    weights = [(1 << 20) // math.isqrt(standing ** lean) + 1 for standing in range(2, count + 1)]
    spare, counts = total - most - (count - 1), [1] * (count - 1)
    while spare > 0:
        movable = [i for i in range(count - 1) if counts[i] < most]
        whole, left = sum([weights[i] for i in movable]), spare
        for i in movable:
            addition = min(most - counts[i], max(1, left * weights[i] // whole), spare)
            counts[i] = counts[i] + addition
            spare = spare - addition
    return np.array([most] + counts)


def ragged(key, amount, total, reach, skew):
    if amount == 2:
        one = jax.random.randint(key, (), max(1, total - reach), min(reach, total - 1) + 1)
        return jnp.stack([one, total - one])
    sizes = jnp.asarray(profile(amount, total, reach, skew), jnp.int32)
    twos = (amount - 1) // 2
    giver, receiver = sizes[1:1 + 2 * twos:2], sizes[2:2 + 2 * twos:2]
    margin = jnp.minimum(giver - 1, reach - receiver)
    shifted = jax.random.randint(jax.random.fold_in(key, 1), (twos,), 0, 1 << 20) % (margin + 1)
    sizes = sizes.at[1:1 + 2 * twos:2].set(giver - shifted).at[2:2 + 2 * twos:2].set(receiver + shifted)
    return sizes[jax.random.permutation(jax.random.fold_in(key, 2), amount)]


def gaussian(stream_key, shape, scale, reach, cuts=(), kind=jnp.bfloat16):
    gain = level_of(stream_key, shape, cuts, -0.22, 0.18) if cuts else 1.0
    values = jax.random.normal(stream_key, shape, jnp.float32) * scale * gain
    return jnp.minimum(jnp.maximum(values, -reach), reach).astype(kind)


def setup_inputs(seed: int = 0) -> dict:
    arg_keys = jax.random.split(jax.random.key(seed), 8)
    tokens = gaussian(arg_keys[0], (TOKENS, D), 1.0, 6.0, ((0, 16),))
    norm_gain = jnp.clip(1.0 + 0.18 * jax.random.normal(arg_keys[1], (D,), jnp.float32), 0.1, 1.9)
    w_query = draw_w_query(jax.random.fold_in(arg_keys[7], 71), 0)
    w_key = draw_w_key(jax.random.fold_in(arg_keys[7], 71), 0)
    w_value = gaussian(arg_keys[4], (D, KVH * HD), D ** -0.5, 0.09375, ((1, 8),))
    w_out = gaussian(arg_keys[5], (H * HD, D), (H * HD // 64) ** -0.5, 0.75, ((0, 8),))
    doc_ids = jnp.searchsorted(jnp.cumsum(ragged(arg_keys[6], DOCS, NB, MAXDOC, 1)), jnp.arange(NB), side="right").astype(jnp.int32)
    return dict(tokens=tokens, norm_gain=norm_gain, w_query=w_query, w_key=w_key, w_value=w_value, w_out=w_out, doc_ids=doc_ids)


floor_score = -1e+30
rope_base = 500000.0
norm_epsilon = 1e-05

def document_starts(doc_ids):
    earlier = doc_ids[None, :] < doc_ids[:, None]
    return lax.optimization_barrier(jnp.sum(earlier.astype(jnp.int32), axis=1)) * BLK

def rotate(values, offsets):
    half_dim = HD // 2
    inverse = jnp.exp(jnp.arange(half_dim, dtype=jnp.float32) * (-2.0 * math.log(rope_base) / HD))
    angles = offsets.astype(jnp.float32)[:, None] * inverse[None, :]
    cos_term = jnp.cos(angles)[:, None, :]
    sin_term = jnp.sin(angles)[:, None, :]
    first_half = values[..., :half_dim]
    second_half = values[..., half_dim:]
    return jnp.concatenate([first_half * cos_term - second_half * sin_term, second_half * cos_term + first_half * sin_term], axis=-1)

def normalize(tokens, norm_gain):
    floats = tokens.astype(jnp.float32)
    squares = lax.optimization_barrier(jnp.mean(floats * floats, axis=-1, keepdims=True))
    return (floats * lax.rsqrt(squares + norm_epsilon) * norm_gain).astype(jnp.bfloat16)

def reference(tokens, norm_gain, w_query, w_key, w_value, w_out, doc_ids):
    normed = normalize(tokens, norm_gain)
    per_group = H // KVH
    query_raw = jnp.dot(normed, w_query, preferred_element_type=jnp.float32)
    key_raw = jnp.dot(normed, w_key, preferred_element_type=jnp.float32)
    values = jnp.dot(normed, w_value, preferred_element_type=jnp.float32).astype(jnp.bfloat16).reshape(TOKENS, KVH, HD)
    token_start = jnp.repeat(document_starts(doc_ids), BLK).astype(jnp.int32)
    positions = jnp.arange(TOKENS, dtype=jnp.int32)
    offsets = positions - token_start
    queries = rotate(query_raw.reshape(TOKENS, H, HD), offsets).astype(jnp.bfloat16)
    keys_rot = rotate(key_raw.reshape(TOKENS, KVH, HD), offsets).astype(jnp.bfloat16)
    window = MAXDOC * BLK
    score_scale = HD ** (-0.5)

    def one_block(block_index):
        first_row = (block_index * BLK).astype(jnp.int32)
        key_first = jnp.clip(first_row + BLK - window, 0, TOKENS - window).astype(jnp.int32)
        query_block = lax.dynamic_slice_in_dim(queries, first_row, BLK, 0).reshape(BLK, KVH, per_group, HD).astype(jnp.float32)
        key_block = lax.dynamic_slice_in_dim(keys_rot, key_first, window, 0).astype(jnp.float32)
        value_block = lax.dynamic_slice_in_dim(values, key_first, window, 0).astype(jnp.float32)
        scores = jnp.einsum('qhgd,khd->hgqk', query_block, key_block) * score_scale
        row_pos = first_row + jnp.arange(BLK, dtype=jnp.int32)
        row_start = lax.dynamic_slice_in_dim(token_start, first_row, BLK, 0)
        key_pos = key_first + jnp.arange(window, dtype=jnp.int32)
        allowed = (key_pos[None, :] >= row_start[:, None]) & (key_pos[None, :] <= row_pos[:, None])
        scores = jnp.where(allowed, scores, floor_score)
        row_max = lax.optimization_barrier(jnp.max(scores, axis=-1, keepdims=True))
        weights = jnp.where(allowed, jnp.exp(scores - row_max), 0.0)
        totals = lax.optimization_barrier(jnp.sum(weights, axis=-1))
        rounded = lax.optimization_barrier(weights.astype(jnp.bfloat16)).astype(jnp.float32)
        context = jnp.einsum('hgqk,khd->qhgd', rounded, value_block) / jnp.transpose(totals, (2, 0, 1))[..., None]
        return context.reshape(BLK, H * HD).astype(jnp.bfloat16)
    context = lax.map(one_block, jnp.arange(NB, dtype=jnp.int32)).reshape(TOKENS, H * HD)
    head_cols = H // N_TP * HD
    summed = jnp.zeros((TOKENS, D), jnp.float32)
    for group_index in range(N_TP):
        group_term = jnp.dot(context[:, group_index * head_cols:(group_index + 1) * head_cols], w_out[group_index * head_cols:(group_index + 1) * head_cols], preferred_element_type=jnp.float32)
        summed = summed + lax.optimization_barrier(group_term.astype(jnp.bfloat16)).astype(jnp.float32)
    return summed.astype(jnp.bfloat16)
```

```python
import functools
import math

import jax
import jax.numpy as jnp
import numpy as np
from jax import lax
from jax.experimental import pallas as pl
from jax.experimental.pallas import tpu as pltpu
from jax.sharding import PartitionSpec as P

HD = 128
BLK = 128
ROWS = 512
BLOCKS = ROWS // BLK
HEADS = 4
REACH = 9
FAR = -1e30
rope_base = 500000.0
norm_epsilon = 1e-05
SCALE = HD ** (-0.5) * math.log2(math.e)


def frequencies():
    half = HD // 2
    inverse = np.exp(np.arange(half, dtype=np.float32) * np.float32(-2.0 * math.log(rope_base) / HD))
    return np.concatenate([inverse, inverse])[None, :].astype(np.float32)


def norm_rows(tok_ref, gain_ref, normed_ref, step):
    rows = pl.ds(pl.multiple_of(step * 16, 16), 16)
    floats = tok_ref[rows, :].astype(jnp.float32)
    mean = jnp.mean(floats * floats, axis=-1, keepdims=True)
    normed_ref[rows, :] = (floats * lax.rsqrt(mean + norm_epsilon) * gain_ref[...]).astype(jnp.bfloat16)


def block_start(doc_ref, block):
    mine = doc_ref[block]

    def count(j, total):
        return total + (doc_ref[j] < mine).astype(jnp.int32)

    return lax.fori_loop(0, doc_ref.shape[0], count, jnp.int32(0), unroll=True) * BLK


def make_tables(doc_ref, freq_ref, cos_ref, sin_ref, shard):
    lane = lax.broadcasted_iota(jnp.int32, (BLK, HD), 1)
    row = lax.broadcasted_iota(jnp.int32, (BLK, HD), 0)
    for b in range(BLOCKS):
        block = shard * BLOCKS + b
        offset = row + (block * BLK - block_start(doc_ref, block))
        angle = offset.astype(jnp.float32) * freq_ref[...]
        rows = pl.ds(b * BLK, BLK)
        cos_ref[rows, :] = jnp.cos(angle)
        sine = jnp.sin(angle)
        sin_ref[rows, :] = jnp.where(lane < HD // 2, -sine, sine)


def rotated(raw, cos, sin):
    return raw * cos + pltpu.roll(raw, HD // 2, 1) * sin


def project_kv(normed_ref, wk_ref, wv_ref, cos_ref, sin_ref, k_ref, v_ref):
    for half in range(2):
        rows = pl.ds(half * 256, 256)
        weights = jnp.concatenate([wk_ref[...], wv_ref[...]], axis=1)
        raw = jnp.dot(normed_ref[rows, :], weights, preferred_element_type=jnp.float32)
        k_ref[rows, :] = rotated(raw[:, :HD], cos_ref[rows, :], sin_ref[rows, :]).astype(jnp.bfloat16)
        v_ref[rows, :] = raw[:, HD:].astype(jnp.bfloat16)


def project_q(normed_ref, wq_ref, cos_ref, sin_ref, q_ref):
    for half in range(2):
        rows = pl.ds(half * 256, 256)
        raw = jnp.dot(normed_ref[rows, :], wq_ref[...], preferred_element_type=jnp.float32)
        cos = cos_ref[rows, :] * SCALE
        sin = sin_ref[rows, :] * SCALE
        for h in range(HEADS):
            out = rotated(raw[:, h * HD:(h + 1) * HD], cos, sin).astype(jnp.bfloat16)
            for b in range(2):
                q_ref[half * 2 + b, h * BLK:(h + 1) * BLK, :] = out[b * BLK:(b + 1) * BLK]


def front_kernel(doc_ref, tok_ref, gain_ref, wq_ref, wk_ref, wv_ref, freq_ref, q_ref, kv_ref, normed_ref, cos_ref, sin_ref):
    shard = lax.axis_index("seq")
    lax.fori_loop(0, ROWS // 16, lambda i, c: (norm_rows(tok_ref, gain_ref, normed_ref, i), c)[1], 0, unroll=2)
    make_tables(doc_ref, freq_ref, cos_ref, sin_ref, shard)
    project_kv(normed_ref, wk_ref, wv_ref, cos_ref, sin_ref, kv_ref.at[:, :HD], kv_ref.at[:, HD:])
    project_q(normed_ref, wq_ref, cos_ref, sin_ref, q_ref)


def query_marks(doc_ref, block):
    lane = lax.broadcasted_iota(jnp.int32, (HEADS * BLK, HD), 1)
    return (lane == doc_ref[block]).astype(jnp.bfloat16)


def key_marks(doc_ref, shard):
    lane = lax.broadcasted_iota(jnp.int32, (BLK, HD), 1)
    return jnp.concatenate(
        [
            jnp.where(lane == doc_ref[shard * BLOCKS + b], 0.0, FAR).astype(jnp.bfloat16)
            for b in range(BLOCKS)
        ],
        axis=0,
    )


def fold(q, keys, values, m_ref, acc_ref, i, rows, first):
    scores = lax.dot_general(q, keys, (((1,), (1,)), ((), ())), preferred_element_type=jnp.float32)
    if first is not None:
        count = scores.shape[0]
        token = lax.broadcasted_iota(jnp.int32, scores.shape, 0) % BLK + first
        key = lax.broadcasted_iota(jnp.int32, scores.shape, 1)
        scores = jnp.where(key <= token, scores, FAR)
        top = jnp.max(scores, axis=1, keepdims=True)
        weights = jnp.exp2(scores - top).astype(jnp.bfloat16)
        acc_ref[i, rows, :] = jnp.dot(weights, values, preferred_element_type=jnp.float32)
        m_ref[i, rows, :] = jnp.broadcast_to(top, (count, HD))
        return
    old = m_ref[i, rows, :]
    new = jnp.maximum(old, jnp.max(scores, axis=1, keepdims=True))
    weights = jnp.exp2(scores - new[:, :1]).astype(jnp.bfloat16)
    factor = jnp.exp2(old - new)
    product = jnp.dot(weights, values, preferred_element_type=jnp.float32)
    acc_ref[i, rows, :] = acc_ref[i, rows, :] * jnp.concatenate([factor, factor], axis=1) + product
    m_ref[i, rows, :] = new


def fold_own(q_ref, marks_ref, keys, values, m_ref, acc_ref):
    for i in range(BLOCKS):
        width = (i + 1) * BLK
        for c in range(2):
            rows = pl.ds(c * 256, 256)
            q = jnp.concatenate([q_ref[i, rows, :], marks_ref[i, rows, :]], axis=1)
            fold(q, keys[:width], values[:width], m_ref, acc_ref, i, rows, i * BLK)


def fold_shard(q_ref, marks_ref, keys, values, m_ref, acc_ref):
    def one(i, carry):
        for c in range(2):
            rows = pl.ds(c * 256, 256)
            q = jnp.concatenate([q_ref[i, rows, :], marks_ref[i, rows, :]], axis=1)
            fold(q, keys, values, m_ref, acc_ref, i, rows, None)
        return carry

    lax.fori_loop(0, BLOCKS, one, 0)


def context_of(acc_ref, i):
    heads = []
    for h in range(HEADS):
        acc = acc_ref[i, h * BLK:(h + 1) * BLK, :]
        heads.append((acc[:, :HD] / acc[:, HD:]).astype(jnp.bfloat16))
    return jnp.concatenate(heads, axis=1)


def back_kernel(doc_ref, q_ref, kv_ref, wo_ref, out_ref, marks_ref, m_ref, acc_ref):
    shard = lax.axis_index("seq")
    for i in range(BLOCKS):
        marks_ref[i] = query_marks(doc_ref, shard * BLOCKS + i)
    ones = jnp.ones((ROWS, HD), jnp.bfloat16)

    def pair(source):
        keys = jnp.concatenate([kv_ref[source, :, :HD], key_marks(doc_ref, source)], axis=1)
        values = jnp.concatenate([kv_ref[source, :, HD:], ones], axis=1)
        return keys, values

    fold_own(q_ref, marks_ref, *pair(shard), m_ref, acc_ref)

    def other(k, carry):
        fold_shard(q_ref, marks_ref, *pair(shard - k), m_ref, acc_ref)
        return carry

    lax.fori_loop(1, jnp.minimum(shard, REACH) + 1, other, 0)

    def project(i, carry):
        rows = pl.ds(pl.multiple_of(i * BLK, BLK), BLK)
        out_ref[rows, :] = jnp.dot(
            context_of(acc_ref, i), wo_ref[...], preferred_element_type=jnp.float32
        ).astype(jnp.bfloat16)
        return carry

    lax.fori_loop(0, BLOCKS, project, 0)


def local(tokens, norm_gain, w_query, w_key, w_value, w_out, doc_ids):
    vmem = pl.BlockSpec(memory_space=pltpu.VMEM)
    smem = pl.BlockSpec(memory_space=pltpu.SMEM)
    params = pltpu.CompilerParams(vmem_limit_bytes=56 * 2**20)
    queries, kv = pl.pallas_call(
        front_kernel,
        out_shape=(
            jax.ShapeDtypeStruct((BLOCKS, HEADS * BLK, HD), jnp.bfloat16),
            jax.ShapeDtypeStruct((ROWS, 2 * HD), jnp.bfloat16),
        ),
        in_specs=[smem] + [vmem] * 6,
        out_specs=(vmem, vmem),
        scratch_shapes=[
            pltpu.VMEM((ROWS, tokens.shape[1]), jnp.bfloat16),
            pltpu.VMEM((ROWS, HD), jnp.float32),
            pltpu.VMEM((ROWS, HD), jnp.float32),
        ],
        compiler_params=params,
    )(doc_ids, tokens, norm_gain[None, :], w_query, w_key, w_value, jnp.asarray(frequencies()))
    gathered = lax.all_gather(kv, "seq", axis=0, tiled=False)
    partial = pl.pallas_call(
        back_kernel,
        out_shape=jax.ShapeDtypeStruct((ROWS, w_out.shape[1]), jnp.bfloat16),
        in_specs=[smem] + [vmem] * 3,
        out_specs=vmem,
        scratch_shapes=[
            pltpu.VMEM((BLOCKS, HEADS * BLK, HD), jnp.bfloat16),
            pltpu.VMEM((BLOCKS, HEADS * BLK, HD), jnp.float32),
            pltpu.VMEM((BLOCKS, HEADS * BLK, 2 * HD), jnp.float32),
        ],
        compiler_params=params,
    )(doc_ids, queries, gathered, w_out)
    return lax.psum_scatter(partial, "tp", scatter_dimension=0, tiled=True)


def solution(mesh):
    placed = (P("seq", None), P(), P(None, "tp"), P(None, "tp"), P(None, "tp"), P("tp", None), P())
    return jax.shard_map(
        local, mesh=mesh, in_specs=placed, out_specs=P(("seq", "tp"), None), check_vma=False
    )
```

```python
import math

import jax
import jax.numpy as jnp
import numpy as np
from jax import lax
from jax.experimental import pallas as pl
from jax.experimental.pallas import tpu as pltpu
from jax.sharding import PartitionSpec as P

HD = 128
BLK = 128
ROWS = 512
BLOCKS = ROWS // BLK
HEADS = 4
PIECES = 2
MESH = pl.DeviceIdType.MESH
FAR = -1e30
rope_base = 500000.0
norm_epsilon = 1e-05
SCALE = HD ** (-0.5) * math.log2(math.e)


def frequencies():
    half = HD // 2
    inverse = np.exp(np.arange(half, dtype=np.float32) * np.float32(-2.0 * math.log(rope_base) / HD))
    return np.concatenate([inverse, inverse])[None, :].astype(np.float32)


def norm_rows(tok_ref, gain_ref, normed_ref, step):
    rows = pl.ds(pl.multiple_of(step * 16, 16), 16)
    floats = tok_ref[rows, :].astype(jnp.float32)
    mean = jnp.mean(floats * floats, axis=-1, keepdims=True)
    normed_ref[rows, :] = (floats * lax.rsqrt(mean + norm_epsilon) * gain_ref[...]).astype(jnp.bfloat16)


def block_start(doc_ref, block):
    mine = doc_ref[block]

    def count(j, total):
        return total + (doc_ref[j] < mine).astype(jnp.int32)

    return lax.fori_loop(0, doc_ref.shape[0], count, jnp.int32(0), unroll=True) * BLK


def make_tables(doc_ref, freq_ref, cos_ref, sin_ref, shard):
    lane = lax.broadcasted_iota(jnp.int32, (BLK, HD), 1)
    row = lax.broadcasted_iota(jnp.int32, (BLK, HD), 0)

    def one(b, carry):
        block = shard * BLOCKS + b
        offset = row + (block * BLK - block_start(doc_ref, block))
        angle = offset.astype(jnp.float32) * freq_ref[...]
        rows = pl.ds(pl.multiple_of(b * BLK, BLK), BLK)
        cos_ref[rows, :] = jnp.cos(angle)
        sine = jnp.sin(angle)
        sin_ref[rows, :] = jnp.where(lane < HD // 2, -sine, sine)
        return carry

    lax.fori_loop(0, BLOCKS, one, 0)


def rotated(raw, cos, sin):
    return raw * cos + pltpu.roll(raw, HD // 2, 1) * sin


def project_kv(normed_ref, wkv_ref, cos_ref, sin_ref, kv_ref):
    for half in range(2):
        rows = pl.ds(half * 256, 256)
        raw = jnp.dot(normed_ref[rows, :], wkv_ref[...], preferred_element_type=jnp.float32)
        kv_ref[rows, :] = rotated(raw[:, :HD], cos_ref[rows, :], sin_ref[rows, :]).astype(jnp.bfloat16)
        for b in range(2):
            at = ROWS + (half * 2 + b) * BLK
            kv_ref[at:at + BLK, :] = raw[b * BLK:(b + 1) * BLK, HD:].T.astype(jnp.bfloat16)


def project_q(normed_ref, wq_ref, cos_ref, sin_ref, q_ref, doc_ref, shard):
    lane = lax.broadcasted_iota(jnp.int32, (HEADS * BLK, HD), 1)
    for half in range(2):
        rows = pl.ds(half * 256, 256)
        raw = jnp.dot(normed_ref[rows, :], wq_ref[...], preferred_element_type=jnp.float32)
        cos = cos_ref[rows, :] * SCALE
        sin = sin_ref[rows, :] * SCALE
        for h in range(HEADS):
            out = rotated(raw[:, h * HD:(h + 1) * HD], cos, sin).astype(jnp.bfloat16)
            for b in range(2):
                q_ref[half * 2 + b, h * BLK:(h + 1) * BLK, :HD] = out[b * BLK:(b + 1) * BLK]
    for i in range(BLOCKS):
        q_ref[i, :, HD:] = (lane == doc_ref[shard * BLOCKS + i]).astype(jnp.bfloat16)


def slot_pair(kv_ref, slot, doc_ref, shard):
    lane = lax.broadcasted_iota(jnp.int32, (BLK, HD), 1)
    marks = [
        jnp.where(lane == doc_ref[shard * BLOCKS + b], 0.0, FAR).astype(jnp.bfloat16)
        for b in range(BLOCKS)
    ]
    keys = jnp.concatenate([kv_ref[slot, :ROWS, :], jnp.concatenate(marks, axis=0)], axis=1)
    columns = [kv_ref[slot, ROWS + b * BLK:ROWS + (b + 1) * BLK, :] for b in range(BLOCKS)]
    values = jnp.concatenate(
        [jnp.concatenate(columns, axis=1), jnp.ones((16, ROWS), jnp.bfloat16)], axis=0
    )
    return keys, values


def scores_of(keys, q):
    return lax.dot_general(keys, q, (((1,), (1,)), ((), ())), preferred_element_type=jnp.float32)


def fold_own(q_ref, keys, values, m_ref, acc_ref):
    token = lax.broadcasted_iota(jnp.int32, (BLK, HEADS * BLK), 1) % BLK
    key = lax.broadcasted_iota(jnp.int32, (BLK, HEADS * BLK), 0)
    causal = key <= token
    for i in range(BLOCKS):
        width = (i + 1) * BLK
        scores = scores_of(keys[:width], q_ref[i])
        last = jnp.where(causal, scores[width - BLK:], FAR)
        scores = last if i == 0 else jnp.concatenate([scores[:width - BLK], last], axis=0)
        top = jnp.max(scores, axis=0, keepdims=True)
        weights = jnp.exp2(scores - top).astype(jnp.bfloat16)
        acc_ref[i] = jnp.dot(values[:, :width], weights, preferred_element_type=jnp.float32)
        m_ref[i, 0:1, :] = top


def fold_shard(q_ref, keys, values, m_ref, acc_ref):
    scores = scores_of(keys, q_ref[0])
    for i in range(BLOCKS):
        following = scores_of(keys, q_ref[i + 1]) if i + 1 < BLOCKS else None
        old = m_ref[i, 0:1, :]
        new = jnp.maximum(old, jnp.max(scores, axis=0, keepdims=True))
        weights = jnp.exp2(scores - new).astype(jnp.bfloat16)
        factor = jnp.exp2(old - new)
        product = jnp.dot(values, weights, preferred_element_type=jnp.float32)
        acc_ref[i] = acc_ref[i] * factor + product
        m_ref[i, 0:1, :] = new
        scores = following


def write_context(acc_ref, i, ctx_ref):
    for h in range(HEADS):
        columns = pl.ds(h * BLK, BLK)
        scaled = acc_ref[i, :HD, columns] / acc_ref[i, HD:HD + 1, columns]
        ctx_ref[:, columns] = scaled.T.astype(jnp.bfloat16)


def kernel(
    doc_ref, tok_hbm, gain_ref, wq_hbm, wk_hbm, wv_hbm, freq_ref, wo_hbm, out_ref,
    tok_ref, wkv_ref, wq_ref, wo_ref, normed_ref, cos_ref, sin_ref, q_ref, kv_ref, m_ref, acc_ref,
    ctx_ref, mine_ref, give_ref, take_ref, pass_ref, half_ref, last_ref,
    load_sem, kv_send, kv_recv, give_send, give_recv, pass_send, half_recv, last_recv,
):
    shard = lax.axis_index("seq")
    part = lax.axis_index("tp")
    z, y = shard // 4, shard % 4
    x, c = part // 2, part % 2

    def at_seq(zz, yy):
        return (((zz + 4) % 4) * 4 + (yy + 4) % 4, part)

    def at_tp(xx, cc):
        return (shard, ((xx + 4) % 4) * 2 + cc)

    loads = []
    for n in range(4):
        rows = pl.ds(n * BLK, BLK)
        loads.append(pltpu.make_async_copy(tok_hbm.at[rows, :], tok_ref.at[rows, :], load_sem.at[n]))
    loads.append(pltpu.make_async_copy(wk_hbm, wkv_ref.at[:, :HD], load_sem.at[4]))
    loads.append(pltpu.make_async_copy(wv_hbm, wkv_ref.at[:, HD:], load_sem.at[5]))
    loads.append(pltpu.make_async_copy(wq_hbm, wq_ref, load_sem.at[6]))
    loads.append(pltpu.make_async_copy(wo_hbm, wo_ref, load_sem.at[7]))
    for load in loads:
        load.start()

    barrier = pltpu.get_barrier_semaphore()
    near = [at_seq(z, y + 1), at_seq(z, y - 1), at_seq(z + 1, y), at_seq(z - 1, y)]
    near += [at_tp(x + 1, c), at_tp(x - 1, c), at_tp(x, 1 - c)]
    for device in near:
        pl.semaphore_signal(barrier, inc=1, device_id=device, device_id_type=MESH)
    first_corner = (z == 0) & (y == 3)
    last_corner = (z == 3) & (y == 0)

    @pl.when(first_corner)
    def _():
        pl.semaphore_signal(barrier, inc=1, device_id=(12, part), device_id_type=MESH)

    @pl.when(last_corner)
    def _():
        pl.semaphore_signal(barrier, inc=1, device_id=(3, part), device_id_type=MESH)

    make_tables(doc_ref, freq_ref, cos_ref, sin_ref, shard)
    for n in range(4):
        loads[n].wait()
        lax.fori_loop(n * 8, n * 8 + 8, lambda i, s: (norm_rows(tok_ref, gain_ref, normed_ref, i), s)[1], 0)
    loads[4].wait()
    loads[5].wait()
    own = y
    project_kv(normed_ref, wkv_ref, cos_ref, sin_ref, kv_ref.at[own])

    pl.semaphore_wait(barrier, len(near) + (first_corner | last_corner).astype(jnp.int32))

    def slot_of(j, step):
        return j * 4 + (y + step + 4) % 4

    def move(name, source, target, device, piece):
        rows = pl.ds(piece * (2 * ROWS // PIECES), 2 * ROWS // PIECES)
        return pltpu.make_async_remote_copy(
            src_ref=kv_ref.at[source, rows, :],
            dst_ref=kv_ref.at[target, rows, :],
            send_sem=kv_send.at[name * PIECES + piece],
            recv_sem=kv_recv.at[target * PIECES + piece],
            device_id=device,
            device_id_type=MESH,
        )

    up, down = at_seq(z, y + 1), at_seq(z, y - 1)
    onward = at_seq(z + 1, y)
    transfers = {}
    for j in range(3):
        transfers["right", j] = (j * 4, slot_of(j, 0), slot_of(j, 0), up)
        transfers["left", j] = (j * 4 + 1, slot_of(j, 0), slot_of(j, 0), down)
        transfers["pass right", j] = (j * 4 + 2, slot_of(j, -1), slot_of(j, -1), up)
        transfers["pass left", j] = (j * 4 + 3, slot_of(j, 1), slot_of(j, 1), down)
    transfers["onward", 0] = (12, slot_of(0, 0), slot_of(1, 0), onward)
    transfers["onward", 1] = (13, slot_of(1, 0), slot_of(2, 0), onward)
    transfers["corner", 0] = (14, slot_of(0, 0), 12, (12, part))
    sends = {
        ("right", 0): y <= 2, ("left", 0): y == 0, ("pass right", 0): y == 2, ("pass left", 0): y == 3,
        ("right", 1): z >= 1, ("left", 1): z >= 1, ("pass left", 1): z >= 1,
        ("right", 2): z >= 2, ("left", 2): (z >= 2) & (y >= 1),
        ("pass right", 2): (z >= 2) & (y == 3), ("pass left", 2): (z >= 2) & (y == 2),
        ("onward", 0): z <= 2, ("onward", 1): (z >= 1) & (z <= 2), ("corner", 0): first_corner,
    }
    arrives = {
        (0, -1): y >= 1, (0, 1): y == 3, (0, 2): y >= 2,
        (1, 0): z >= 1, (1, -1): z >= 1, (1, 1): z >= 1, (1, 2): z >= 1,
        (2, 0): z >= 2, (2, -1): z >= 2, (2, 1): (z >= 2) & (y <= 2), (2, 2): (z >= 2) & (y <= 1),
        (3, 0): last_corner,
    }

    def start(*keys):
        for key in keys:
            @pl.when(sends[key])
            def _(key=key):
                for piece in range(PIECES):
                    move(*transfers[key], piece).start()

    def arrive(key, *then):
        j, step = key
        slot = 12 if j == 3 else slot_of(j, step)

        @pl.when(arrives[key])
        def _():
            for piece in range(PIECES):
                move(0, slot, slot, up, piece).wait_recv()
                for other in then:
                    @pl.when(sends[other])
                    def _(other=other):
                        move(*transfers[other], piece).start()

    start(("onward", 0), ("right", 0), ("left", 0), ("corner", 0))
    loads[6].wait()
    project_q(normed_ref, wq_ref, cos_ref, sin_ref, q_ref, doc_ref, shard)
    fold_own(q_ref, *slot_pair(kv_ref, own, doc_ref, shard), m_ref, acc_ref)

    order = [
        ((0, -1), [((1, 0), ("onward", 1), ("right", 1), ("left", 1)), ((0, -1), ("pass right", 0))]),
        ((1, 0), [((0, 1), ("pass left", 0))]),
        ((0, 1), []),
        ((1, 1), [((2, 0), ("right", 2), ("left", 2)), ((1, 1), ("pass left", 1))]),
        ((0, 2), [((0, 2),)]),
        ((1, -1), [((1, -1),)]),
        ((2, 0), [((2, -1), ("pass right", 2)), ((2, 1), ("pass left", 2))]),
        ((2, -1), []),
        ((2, 1), []),
        ((1, 2), [((1, 2),)]),
        ((2, 2), [((2, 2),)]),
        ((3, 0), [((3, 0),)]),
    ]

    def step(k, carry):
        row, turn, valid = jnp.int32(0), jnp.int32(0), jnp.int32(0)
        for n, (key, events) in enumerate(order):
            if events:
                @pl.when(k == n)
                def _(events=events):
                    for event in events:
                        arrive(*event)
            here = k == n
            row = jnp.where(here, key[0], row)
            turn = jnp.where(here, (y + key[1] + 4) % 4, turn)
            valid = jnp.where(here, arrives[key].astype(jnp.int32), valid)
        corner = row == 3
        slot = jnp.where(corner, 12, row * 4 + turn)
        source = jnp.where(corner, 3, (z - row) * 4 + turn)

        @pl.when(valid == 1)
        def _():
            fold_shard(q_ref, *slot_pair(kv_ref, slot, doc_ref, source), m_ref, acc_ref)

        return carry

    lax.fori_loop(0, len(order), step, 0)
    for key in sends:
        @pl.when(sends[key])
        def _(key=key):
            for piece in range(PIECES):
                move(*transfers[key], piece).wait_send()

    loads[7].wait()
    half = wo_ref.shape[1] // 2

    def give(k):
        return pltpu.make_async_remote_copy(
            src_ref=give_ref.at[k], dst_ref=take_ref.at[k], send_sem=give_send.at[k], recv_sem=give_recv.at[k],
            device_id=at_tp(x, 1 - c), device_id_type=MESH,
        )

    def halves(h):
        return pltpu.make_async_remote_copy(
            src_ref=pass_ref.at[0, h], dst_ref=half_ref.at[h], send_sem=pass_send.at[h], recv_sem=half_recv.at[h],
            device_id=at_tp(x + 1 - 2 * h, c), device_id_type=MESH,
        )

    def lasts(k):
        return pltpu.make_async_remote_copy(
            src_ref=pass_ref.at[k], dst_ref=last_ref.at[k - 1], send_sem=pass_send.at[1 + k], recv_sem=last_recv.at[k - 1],
            device_id=at_tp(x + 3 - 2 * k, c), device_id_type=MESH,
        )

    def project(k, carry):
        i = jnp.where(k == 0, x + 2, jnp.where(k == 1, x + 1, jnp.where(k == 2, x + 3, x))) % 4
        write_context(acc_ref, i, ctx_ref)
        theirs = ctx_ref[pl.ds(pl.multiple_of((1 - c) * 64, 64), 64), :]
        ours = ctx_ref[pl.ds(pl.multiple_of(c * 64, 64), 64), :]
        both = jnp.concatenate([theirs, ours], axis=0)
        product = jnp.dot(both, wo_ref[...], preferred_element_type=jnp.float32)
        for h in range(2):
            columns = slice(h * half, (h + 1) * half)
            give_ref[k, h] = product[:64, columns].astype(jnp.bfloat16)
            mine_ref[k, h] = product[64:, columns]
        give(k).start()
        return carry

    def paired(k, h):
        return mine_ref[k, h] + take_ref[k, h].astype(jnp.float32)

    lax.fori_loop(0, 2, project, 0)
    give(0).wait_recv()
    for h in range(2):
        pass_ref[0, h] = paired(0, h).astype(jnp.bfloat16)
        halves(h).start()
    lax.fori_loop(2, 4, project, 0)
    for k in (1, 2):
        give(k).wait_recv()
        halves(k - 1).wait_recv()
        for h in range(2):
            total = paired(k, h)
            if h == k - 1:
                total = total + half_ref[h].astype(jnp.float32)
            pass_ref[k, h] = total.astype(jnp.bfloat16)
        lasts(k).start()
    give(3).wait_recv()
    for h in range(2):
        mine_ref[3, h] = paired(3, h)
    lasts(1).wait_recv()
    lasts(2).wait_recv()
    for h in range(2):
        total = mine_ref[3, h] + last_ref[0, h].astype(jnp.float32) + last_ref[1, h].astype(jnp.float32)
        out_ref[:, h * half:(h + 1) * half] = total.astype(jnp.bfloat16)
    for k in range(4):
        give(k).wait_send()
    for h in range(2):
        halves(h).wait_send()
        lasts(h + 1).wait_send()


def local(tokens, norm_gain, w_query, w_key, w_value, w_out, doc_ids):
    vmem = pl.BlockSpec(memory_space=pltpu.VMEM)
    smem = pl.BlockSpec(memory_space=pltpu.SMEM)
    hbm = pl.BlockSpec(memory_space=pl.ANY)
    width = tokens.shape[1]
    half = w_out.shape[1] // 2
    b16, f32 = jnp.bfloat16, jnp.float32
    dma = pltpu.SemaphoreType.DMA
    return pl.pallas_call(
        kernel,
        out_shape=jax.ShapeDtypeStruct((64, w_out.shape[1]), b16),
        in_specs=[smem, hbm, vmem, hbm, hbm, hbm, vmem, hbm],
        out_specs=vmem,
        scratch_shapes=[
            pltpu.VMEM((ROWS, width), b16),
            pltpu.VMEM((width, 2 * HD), b16),
            pltpu.VMEM((width, HEADS * HD), b16),
            pltpu.VMEM((HEADS * HD, w_out.shape[1]), b16),
            pltpu.VMEM((ROWS, width), b16),
            pltpu.VMEM((ROWS, HD), f32),
            pltpu.VMEM((ROWS, HD), f32),
            pltpu.VMEM((BLOCKS, HEADS * BLK, 2 * HD), b16),
            pltpu.VMEM((13, 2 * ROWS, HD), b16),
            pltpu.VMEM((BLOCKS, 8, HEADS * BLK), f32),
            pltpu.VMEM((BLOCKS, HD + 16, HEADS * BLK), f32),
            pltpu.VMEM((BLK, HEADS * HD), b16),
            pltpu.VMEM((4, 2, 64, half), f32),
            pltpu.VMEM((4, 2, 64, half), b16),
            pltpu.VMEM((4, 2, 64, half), b16),
            pltpu.VMEM((3, 2, 64, half), b16),
            pltpu.VMEM((2, 64, half), b16),
            pltpu.VMEM((2, 2, 64, half), b16),
            dma((8,)), dma((15 * PIECES,)), dma((13 * PIECES,)), dma((4,)), dma((4,)), dma((4,)), dma((2,)), dma((2,)),
        ],
        compiler_params=pltpu.CompilerParams(
            vmem_limit_bytes=58 * 2**20, collective_id=0, has_side_effects=True
        ),
        cost_estimate=pl.CostEstimate(flops=10**10, bytes_accessed=15 * 2**20, transcendentals=10**7),
    )(doc_ids, tokens, norm_gain[None, :], w_query, w_key, w_value, jnp.asarray(frequencies()), w_out)


def solution(mesh):
    placed = (P("seq", None), P(), P(None, "tp"), P(None, "tp"), P(None, "tp"), P("tp", None), P())
    return jax.shard_map(
        local, mesh=mesh, in_specs=placed, out_specs=P(("seq", "tp"), None), check_vma=False
    )
```

```python
import math

import jax
import jax.numpy as jnp
import numpy as np
from jax import lax
from jax.experimental import pallas as pl
from jax.experimental.pallas import tpu as pltpu
from jax.sharding import PartitionSpec as P

HD = 128
BLK = 128
ROWS = 512
BLOCKS = ROWS // BLK
HEADS = 4
PIECES = 2
NORM_ROWS = 32
MESH = pl.DeviceIdType.MESH
FAR = -1e30
rope_base = 500000.0
norm_epsilon = 1e-05
SCALE = HD ** (-0.5) * math.log2(math.e)


def frequencies():
    half = HD // 2
    inverse = np.exp(np.arange(half, dtype=np.float32) * np.float32(-2.0 * math.log(rope_base) / HD))
    return np.concatenate([inverse, inverse])[None, :].astype(np.float32)


def norm_rows(tok_ref, gain_ref, normed_ref, step):
    rows = pl.ds(pl.multiple_of(step * NORM_ROWS, NORM_ROWS), NORM_ROWS)
    width = tok_ref.shape[1]
    squares = jnp.zeros((NORM_ROWS, HD), jnp.float32)
    for at in range(0, width, HD):
        floats = tok_ref[rows, at:at + HD].astype(jnp.float32)
        squares = squares + floats * floats
    mean = jnp.sum(squares, axis=1, keepdims=True) * (1.0 / width)
    factor = lax.rsqrt(mean + norm_epsilon)
    for at in range(0, width, HD):
        floats = tok_ref[rows, at:at + HD].astype(jnp.float32)
        normed_ref[rows, at:at + HD] = (floats * factor * gain_ref[:, at:at + HD]).astype(jnp.bfloat16)


def block_start(doc_ref, block):
    mine = doc_ref[block]

    def count(j, total):
        return total + (doc_ref[j] < mine).astype(jnp.int32)

    return lax.fori_loop(0, doc_ref.shape[0], count, jnp.int32(0), unroll=True) * BLK


def make_tables(doc_ref, freq_ref, cos_ref, sin_ref, shard):
    lane = lax.broadcasted_iota(jnp.int32, (BLK, HD), 1)
    row = lax.broadcasted_iota(jnp.int32, (BLK, HD), 0)

    def one(b, carry):
        block = shard * BLOCKS + b
        offset = row + (block * BLK - block_start(doc_ref, block))
        angle = offset.astype(jnp.float32) * freq_ref[...]
        rows = pl.ds(pl.multiple_of(b * BLK, BLK), BLK)
        cos_ref[rows, :] = jnp.cos(angle)
        sine = jnp.sin(angle)
        sin_ref[rows, :] = jnp.where(lane < HD // 2, -sine, sine)
        return carry

    lax.fori_loop(0, BLOCKS, one, 0)


def rotated(raw, cos, sin):
    return raw * cos + pltpu.roll(raw, HD // 2, 1) * sin


def project_kv(normed_ref, wkv_ref, cos_ref, sin_ref, kv_ref, half):
    rows = pl.ds(half * 256, 256)
    raw = jnp.dot(normed_ref[rows, :], wkv_ref[...], preferred_element_type=jnp.float32)
    keys = rotated(raw[:, :HD], cos_ref[rows, :], sin_ref[rows, :]).astype(jnp.bfloat16)
    for b in range(2):
        at = (half * 2 + b) * 2 * BLK
        kv_ref[at:at + BLK, :] = keys[b * BLK:(b + 1) * BLK]
        kv_ref[at + BLK:at + 2 * BLK, :] = raw[b * BLK:(b + 1) * BLK, HD:].T.astype(jnp.bfloat16)


def project_q(normed_ref, wq_ref, cos_ref, sin_ref, q_ref, doc_ref, shard):
    lane = lax.broadcasted_iota(jnp.int32, (HEADS * BLK, HD), 1)
    for half in range(2):
        rows = pl.ds(half * 256, 256)
        raw = jnp.dot(normed_ref[rows, :], wq_ref[...], preferred_element_type=jnp.float32)
        cos = cos_ref[rows, :] * SCALE
        sin = sin_ref[rows, :] * SCALE
        for h in range(HEADS):
            out = rotated(raw[:, h * HD:(h + 1) * HD], cos, sin).astype(jnp.bfloat16)
            for b in range(2):
                q_ref[half * 2 + b, h * BLK:(h + 1) * BLK, :HD] = out[b * BLK:(b + 1) * BLK]
    for i in range(BLOCKS):
        q_ref[i, :, HD:] = (lane == doc_ref[shard * BLOCKS + i]).astype(jnp.bfloat16)


def slot_pair(kv_ref, slot, doc_ref, shard):
    lane = lax.broadcasted_iota(jnp.int32, (BLK, HD), 1)
    marks = [
        jnp.where(lane == doc_ref[shard * BLOCKS + b], 0.0, FAR).astype(jnp.bfloat16)
        for b in range(BLOCKS)
    ]
    pieces = [kv_ref[slot, 2 * b * BLK:(2 * b + 1) * BLK, :] for b in range(BLOCKS)]
    keys = jnp.concatenate([jnp.concatenate(pieces, axis=0), jnp.concatenate(marks, axis=0)], axis=1)
    columns = [kv_ref[slot, (2 * b + 1) * BLK:(2 * b + 2) * BLK, :] for b in range(BLOCKS)]
    values = jnp.concatenate(
        [jnp.concatenate(columns, axis=1), jnp.ones((16, ROWS), jnp.bfloat16)], axis=0
    )
    return keys, values


def scores_of(keys, q):
    return lax.dot_general(keys, q, (((1,), (1,)), ((), ())), preferred_element_type=jnp.float32)


def fold_own(q_ref, keys, values, m_ref, acc_ref):
    token = lax.broadcasted_iota(jnp.int32, (BLK, HEADS * BLK), 1) % BLK
    key = lax.broadcasted_iota(jnp.int32, (BLK, HEADS * BLK), 0)
    causal = key <= token
    for i in range(BLOCKS):
        width = (i + 1) * BLK
        scores = scores_of(keys[:width], q_ref[i])
        last = jnp.where(causal, scores[width - BLK:], FAR)
        scores = last if i == 0 else jnp.concatenate([scores[:width - BLK], last], axis=0)
        top = jnp.max(scores, axis=0, keepdims=True)
        weights = jnp.exp2(scores - top).astype(jnp.bfloat16)
        acc_ref[i] = jnp.dot(values[:, :width], weights, preferred_element_type=jnp.float32)
        m_ref[i, 0:1, :] = top


def fold_shard(q_ref, keys, values, m_ref, acc_ref):
    scores = scores_of(keys, q_ref[0])
    for i in range(BLOCKS):
        following = scores_of(keys, q_ref[i + 1]) if i + 1 < BLOCKS else None
        old = m_ref[i, 0:1, :]
        new = jnp.maximum(old, jnp.max(scores, axis=0, keepdims=True))
        weights = jnp.exp2(scores - new).astype(jnp.bfloat16)
        factor = jnp.exp2(old - new)
        product = jnp.dot(values, weights, preferred_element_type=jnp.float32)
        acc_ref[i] = acc_ref[i] * factor + product
        m_ref[i, 0:1, :] = new
        scores = following


def write_context(acc_ref, i, ctx_ref):
    for h in range(HEADS):
        columns = pl.ds(h * BLK, BLK)
        scaled = acc_ref[i, :HD, columns] / acc_ref[i, HD:HD + 1, columns]
        ctx_ref[:, columns] = scaled.T.astype(jnp.bfloat16)


def kernel(
    doc_ref, tok_hbm, gain_ref, wq_hbm, wk_hbm, wv_hbm, freq_ref, wo_hbm, out_ref,
    tok_ref, wkv_ref, wq_ref, wo_ref, normed_ref, cos_ref, sin_ref, q_ref, kv_ref, m_ref, acc_ref,
    ctx_ref, mine_ref, give_ref, take_ref, pass_ref, half_ref, last_ref,
    load_sem, kv_send, kv_recv, give_send, give_recv, pass_send, half_recv, last_recv,
):
    shard = lax.axis_index("seq")
    part = lax.axis_index("tp")
    z, y = shard // 4, shard % 4
    x, c = part // 2, part % 2

    def at_seq(zz, yy):
        return (((zz + 4) % 4) * 4 + (yy + 4) % 4, part)

    def at_tp(xx, cc):
        return (shard, ((xx + 4) % 4) * 2 + cc)

    loads = []
    for n in range(4):
        rows = pl.ds(n * BLK, BLK)
        loads.append(pltpu.make_async_copy(tok_hbm.at[rows, :], tok_ref.at[rows, :], load_sem.at[n]))
    loads.append(pltpu.make_async_copy(wk_hbm, wkv_ref.at[:, :HD], load_sem.at[4]))
    loads.append(pltpu.make_async_copy(wv_hbm, wkv_ref.at[:, HD:], load_sem.at[5]))
    loads.append(pltpu.make_async_copy(wq_hbm, wq_ref, load_sem.at[6]))
    loads.append(pltpu.make_async_copy(wo_hbm, wo_ref, load_sem.at[7]))
    for n in (0, 4, 5, 1, 2, 3):
        loads[n].start()

    barrier = pltpu.get_barrier_semaphore()
    near = [at_seq(z, y + 1), at_seq(z, y - 1), at_seq(z + 1, y), at_seq(z - 1, y)]
    near += [at_tp(x + 1, c), at_tp(x - 1, c), at_tp(x, 1 - c)]
    for device in near:
        pl.semaphore_signal(barrier, inc=1, device_id=device, device_id_type=MESH)
    first_corner = (z == 0) & (y == 3)
    last_corner = (z == 3) & (y == 0)

    @pl.when(first_corner)
    def _():
        pl.semaphore_signal(barrier, inc=1, device_id=(12, part), device_id_type=MESH)

    @pl.when(last_corner)
    def _():
        pl.semaphore_signal(barrier, inc=1, device_id=(3, part), device_id_type=MESH)

    make_tables(doc_ref, freq_ref, cos_ref, sin_ref, shard)
    def slot_of(j, step):
        return j * 4 + (y + step + 4) % 4

    def move(name, source, target, device, piece):
        rows = pl.ds(piece * (2 * ROWS // PIECES), 2 * ROWS // PIECES)
        return pltpu.make_async_remote_copy(
            src_ref=kv_ref.at[source, rows, :],
            dst_ref=kv_ref.at[target, rows, :],
            send_sem=kv_send.at[name * PIECES + piece],
            recv_sem=kv_recv.at[target * PIECES + piece],
            device_id=device,
            device_id_type=MESH,
        )

    up, down = at_seq(z, y + 1), at_seq(z, y - 1)
    onward = at_seq(z + 1, y)
    transfers = {}
    for j in range(3):
        transfers["right", j] = (j * 4, slot_of(j, 0), slot_of(j, 0), up)
        transfers["left", j] = (j * 4 + 1, slot_of(j, 0), slot_of(j, 0), down)
        transfers["pass right", j] = (j * 4 + 2, slot_of(j, -1), slot_of(j, -1), up)
        transfers["pass left", j] = (j * 4 + 3, slot_of(j, 1), slot_of(j, 1), down)
    transfers["onward", 0] = (12, slot_of(0, 0), slot_of(1, 0), onward)
    transfers["onward", 1] = (13, slot_of(1, 0), slot_of(2, 0), onward)
    transfers["beside", 0] = (14, slot_of(0, -1), slot_of(1, -1), onward)
    transfers["corner", 0] = (15, slot_of(0, 0), 12, (12, part))
    sends = {
        ("right", 0): y <= 2, ("left", 0): y == 0, ("pass right", 0): y == 2, ("pass left", 0): y == 3,
        ("right", 1): (z >= 1) & (y == 3), ("left", 1): z >= 1,
        ("pass right", 1): (z >= 1) & (y != 2), ("pass left", 1): (z >= 1) & (y == 0),
        ("right", 2): z >= 2, ("left", 2): (z >= 2) & (y >= 1),
        ("pass left", 2): (z >= 2) & ((y == 1) | (y == 2)),
        ("onward", 0): z <= 2, ("onward", 1): (z >= 1) & (z <= 2), ("beside", 0): (z <= 2) & (y >= 1),
        ("corner", 0): first_corner,
    }
    arrives = {
        (0, -1): y >= 1, (0, 1): y == 3, (0, 2): y >= 2,
        (1, 0): z >= 1, (1, -1): z >= 1, (1, 1): z >= 1, (1, 2): z >= 1,
        (2, 0): z >= 2, (2, -1): z >= 2, (2, 1): (z >= 2) & (y <= 2), (2, 2): (z >= 2) & (y <= 1),
        (3, 0): last_corner,
    }

    def start(key, piece):
        @pl.when(sends[key])
        def _():
            move(*transfers[key], piece).start()

    def arrive(events):
        for piece in range(PIECES):
            for key, *then in events:
                j, step = key
                slot = 12 if j == 3 else slot_of(j, step)

                @pl.when(arrives[key])
                def _(slot=slot, then=then):
                    move(0, slot, slot, up, piece).wait_recv()
                    for other in then:
                        start(other, piece)

    own = y
    per = BLK // NORM_ROWS
    for piece in range(PIECES):
        for n in (2 * piece, 2 * piece + 1):
            loads[n].wait()
            if n == 3:
                loads[6].start()
                loads[7].start()
            lax.fori_loop(
                n * per, n * per + per, lambda i, s: (norm_rows(tok_ref, gain_ref, normed_ref, i), s)[1], 0
            )
        if piece == 0:
            loads[4].wait()
            loads[5].wait()
        project_kv(normed_ref, wkv_ref, cos_ref, sin_ref, kv_ref.at[own], piece)
        if piece == 0:
            pl.semaphore_wait(barrier, len(near) + (first_corner | last_corner).astype(jnp.int32))
        for key in (("onward", 0), ("right", 0), ("left", 0), ("corner", 0)):
            start(key, piece)

    loads[6].wait()
    project_q(normed_ref, wq_ref, cos_ref, sin_ref, q_ref, doc_ref, shard)
    fold_own(q_ref, *slot_pair(kv_ref, own, doc_ref, shard), m_ref, acc_ref)

    order = [
        ((0, -1), [
            ((1, 0), ("onward", 1), ("left", 1), ("right", 1)),
            ((0, -1), ("pass right", 0), ("beside", 0)),
            ((0, 1), ("pass left", 0)),
        ]),
        ((1, 0), []),
        ((0, 1), []),
        ((1, 1), [((2, 0), ("left", 2), ("right", 2)), ((1, 1), ("pass left", 1))]),
        ((0, 2), [((0, 2),)]),
        ((2, 0), []),
        ((1, -1), [((2, 1), ("pass left", 2)), ((1, -1), ("pass right", 1))]),
        ((2, 1), []),
        ((2, -1), [((2, -1),)]),
        ((1, 2), [((1, 2),)]),
        ((2, 2), [((2, 2),)]),
        ((3, 0), [((3, 0),)]),
    ]

    def step(k, carry):
        row, turn, valid = jnp.int32(0), jnp.int32(0), jnp.int32(0)
        for n, (key, events) in enumerate(order):
            if events:
                @pl.when(k == n)
                def _(events=events):
                    arrive(events)
            here = k == n
            row = jnp.where(here, key[0], row)
            turn = jnp.where(here, (y + key[1] + 4) % 4, turn)
            valid = jnp.where(here, arrives[key].astype(jnp.int32), valid)
        corner = row == 3
        slot = jnp.where(corner, 12, row * 4 + turn)
        source = jnp.where(corner, 3, (z - row) * 4 + turn)

        @pl.when(valid == 1)
        def _():
            fold_shard(q_ref, *slot_pair(kv_ref, slot, doc_ref, source), m_ref, acc_ref)

        return carry

    lax.fori_loop(0, len(order), step, 0)
    for key in sends:
        @pl.when(sends[key])
        def _(key=key):
            for piece in range(PIECES):
                move(*transfers[key], piece).wait_send()

    loads[7].wait()
    half = wo_ref.shape[1] // 2

    def give(k, h):
        return pltpu.make_async_remote_copy(
            src_ref=give_ref.at[k, h], dst_ref=take_ref.at[k, h],
            send_sem=give_send.at[2 * k + h], recv_sem=give_recv.at[2 * k + h],
            device_id=at_tp(x, 1 - c), device_id_type=MESH,
        )

    def first(h):
        return pltpu.make_async_remote_copy(
            src_ref=pass_ref.at[0, h], dst_ref=half_ref.at[h], send_sem=pass_send.at[h], recv_sem=half_recv.at[h],
            device_id=at_tp(x + 1 - 2 * h, c), device_id_type=MESH,
        )

    def final(k, h):
        return pltpu.make_async_remote_copy(
            src_ref=pass_ref.at[k, h], dst_ref=last_ref.at[k - 1, h],
            send_sem=pass_send.at[2 * k + h], recv_sem=last_recv.at[2 * k - 2 + h],
            device_id=at_tp(x + 3 - 2 * k, c), device_id_type=MESH,
        )

    targets = [(x + 2) % 4, (x + 1) % 4, (x + 3) % 4, x]

    def context(k):
        write_context(acc_ref, targets[k], ctx_ref.at[k])

    def project(k, h):
        theirs = ctx_ref[k, pl.ds(pl.multiple_of((1 - c) * 64, 64), 64), :]
        ours = ctx_ref[k, pl.ds(pl.multiple_of(c * 64, 64), 64), :]
        both = jnp.concatenate([theirs, ours], axis=0)
        product = jnp.dot(both, wo_ref[:, h * half:(h + 1) * half], preferred_element_type=jnp.float32)
        give_ref[k, h] = product[:64].astype(jnp.bfloat16)
        give(k, h).start()
        mine_ref[k, h] = product[64:]

    def paired(k, h):
        give(k, h).wait_recv()
        return mine_ref[k, h] + take_ref[k, h].astype(jnp.float32)

    def send_first(h):
        pass_ref[0, h] = paired(0, h).astype(jnp.bfloat16)
        first(h).start()

    def send_final(k, h, forward):
        total = paired(k, h)
        if forward:
            first(h).wait_recv()
            total = total + half_ref[h].astype(jnp.float32)
        pass_ref[k, h] = total.astype(jnp.bfloat16)
        final(k, h).start()

    context(0)
    project(0, 0)
    project(0, 1)
    context(1)
    send_first(0)
    project(1, 1)
    send_first(1)
    context(2)
    project(2, 0)
    send_final(1, 1, False)
    project(1, 0)
    send_final(2, 0, False)
    project(2, 1)
    context(3)
    project(3, 0)
    project(3, 1)
    send_final(1, 0, True)
    send_final(2, 1, True)
    for h in range(2):
        early = 2 - h
        total = paired(3, h)
        final(early, h).wait_recv()
        mine_ref[3, h] = total + last_ref[early - 1, h].astype(jnp.float32)
    for h in range(2):
        late = 1 + h
        final(late, h).wait_recv()
        total = mine_ref[3, h] + last_ref[late - 1, h].astype(jnp.float32)
        out_ref[:, h * half:(h + 1) * half] = total.astype(jnp.bfloat16)
    for h in range(2):
        for k in range(4):
            give(k, h).wait_send()
        first(h).wait_send()
        final(1, h).wait_send()
        final(2, h).wait_send()


def local(tokens, norm_gain, w_query, w_key, w_value, w_out, doc_ids):
    vmem = pl.BlockSpec(memory_space=pltpu.VMEM)
    smem = pl.BlockSpec(memory_space=pltpu.SMEM)
    hbm = pl.BlockSpec(memory_space=pl.ANY)
    width = tokens.shape[1]
    half = w_out.shape[1] // 2
    b16, f32 = jnp.bfloat16, jnp.float32
    dma = pltpu.SemaphoreType.DMA
    return pl.pallas_call(
        kernel,
        out_shape=jax.ShapeDtypeStruct((64, w_out.shape[1]), b16),
        in_specs=[smem, hbm, vmem, hbm, hbm, hbm, vmem, hbm],
        out_specs=vmem,
        scratch_shapes=[
            pltpu.VMEM((ROWS, width), b16),
            pltpu.VMEM((width, 2 * HD), b16),
            pltpu.VMEM((width, HEADS * HD), b16),
            pltpu.VMEM((HEADS * HD, w_out.shape[1]), b16),
            pltpu.VMEM((ROWS, width), b16),
            pltpu.VMEM((ROWS, HD), f32),
            pltpu.VMEM((ROWS, HD), f32),
            pltpu.VMEM((BLOCKS, HEADS * BLK, 2 * HD), b16),
            pltpu.VMEM((13, 2 * ROWS, HD), b16),
            pltpu.VMEM((BLOCKS, 8, HEADS * BLK), f32),
            pltpu.VMEM((BLOCKS, HD + 16, HEADS * BLK), f32),
            pltpu.VMEM((4, BLK, HEADS * HD), b16),
            pltpu.VMEM((4, 2, 64, half), f32),
            pltpu.VMEM((4, 2, 64, half), b16),
            pltpu.VMEM((4, 2, 64, half), b16),
            pltpu.VMEM((3, 2, 64, half), b16),
            pltpu.VMEM((2, 64, half), b16),
            pltpu.VMEM((2, 2, 64, half), b16),
            dma((8,)), dma((16 * PIECES,)), dma((13 * PIECES,)), dma((8,)), dma((8,)), dma((6,)), dma((2,)), dma((4,)),
        ],
        compiler_params=pltpu.CompilerParams(
            vmem_limit_bytes=58 * 2**20, collective_id=0, has_side_effects=True
        ),
        cost_estimate=pl.CostEstimate(flops=10**10, bytes_accessed=15 * 2**20, transcendentals=10**7),
    )(doc_ids, tokens, norm_gain[None, :], w_query, w_key, w_value, jnp.asarray(frequencies()), w_out)


def solution(mesh):
    placed = (P("seq", None), P(), P(None, "tp"), P(None, "tp"), P(None, "tp"), P("tp", None), P())
    return jax.shard_map(
        local, mesh=mesh, in_specs=placed, out_specs=P(("seq", "tp"), None), check_vma=False
    )
```

```python
import math

import jax
import jax.numpy as jnp
import numpy as np
from jax import lax
from jax.experimental import pallas as pl
from jax.experimental.pallas import tpu as pltpu
from jax.sharding import PartitionSpec as P

HD = 128
BLK = 128
ROWS = 512
BLOCKS = ROWS // BLK
HEADS = 4
PIECES = 2
CUTS = 8
NORM_ROWS = 32
MESH = pl.DeviceIdType.MESH
FAR = -1e30
rope_base = 500000.0
norm_epsilon = 1e-05
SCALE = HD ** (-0.5) * math.log2(math.e)


def frequencies():
    half = HD // 2
    inverse = np.exp(np.arange(half, dtype=np.float32) * np.float32(-2.0 * math.log(rope_base) / HD))
    return np.concatenate([inverse, inverse])[None, :].astype(np.float32)


def norm_rows(tok_ref, gain_ref, normed_ref, step):
    rows = pl.ds(pl.multiple_of(step * NORM_ROWS, NORM_ROWS), NORM_ROWS)
    width = tok_ref.shape[1]
    squares = jnp.zeros((NORM_ROWS, HD), jnp.float32)
    for at in range(0, width, HD):
        floats = tok_ref[rows, at:at + HD].astype(jnp.float32)
        squares = squares + floats * floats
    mean = jnp.sum(squares, axis=1, keepdims=True) * (1.0 / width)
    factor = lax.rsqrt(mean + norm_epsilon)
    for at in range(0, width, HD):
        floats = tok_ref[rows, at:at + HD].astype(jnp.float32)
        normed_ref[rows, at:at + HD] = (floats * factor * gain_ref[:, at:at + HD]).astype(jnp.bfloat16)


def block_start(doc_ref, block):
    mine = doc_ref[block]

    def count(j, total):
        return total + (doc_ref[j] < mine).astype(jnp.int32)

    return lax.fori_loop(0, doc_ref.shape[0], count, jnp.int32(0), unroll=True) * BLK


def make_tables(doc_ref, freq_ref, cos_ref, sin_ref, shard):
    lane = lax.broadcasted_iota(jnp.int32, (BLK, HD), 1)
    row = lax.broadcasted_iota(jnp.int32, (BLK, HD), 0)

    def one(b, carry):
        block = shard * BLOCKS + b
        offset = row + (block * BLK - block_start(doc_ref, block))
        angle = offset.astype(jnp.float32) * freq_ref[...]
        rows = pl.ds(pl.multiple_of(b * BLK, BLK), BLK)
        cos_ref[rows, :] = jnp.cos(angle)
        sine = jnp.sin(angle)
        sin_ref[rows, :] = jnp.where(lane < HD // 2, -sine, sine)
        return carry

    lax.fori_loop(0, BLOCKS, one, 0)


def rotated(raw, cos, sin):
    return raw * cos + pltpu.roll(raw, HD // 2, 1) * sin


def project_kv(normed_ref, wkv_ref, cos_ref, sin_ref, kv_ref, half):
    rows = pl.ds(half * 256, 256)
    raw = jnp.dot(normed_ref[rows, :], wkv_ref[...], preferred_element_type=jnp.float32)
    keys = rotated(raw[:, :HD], cos_ref[rows, :], sin_ref[rows, :]).astype(jnp.bfloat16)
    for b in range(2):
        at = (half * 2 + b) * 2 * BLK
        kv_ref[at:at + BLK, :] = keys[b * BLK:(b + 1) * BLK]
        kv_ref[at + BLK:at + 2 * BLK, :] = raw[b * BLK:(b + 1) * BLK, HD:].T.astype(jnp.bfloat16)


def project_q(normed_ref, wq_ref, cos_ref, sin_ref, q_ref, doc_ref, shard):
    lane = lax.broadcasted_iota(jnp.int32, (HEADS * BLK, HD), 1)
    for half in range(2):
        rows = pl.ds(half * 256, 256)
        raw = jnp.dot(normed_ref[rows, :], wq_ref[...], preferred_element_type=jnp.float32)
        cos = cos_ref[rows, :] * SCALE
        sin = sin_ref[rows, :] * SCALE
        for h in range(HEADS):
            out = rotated(raw[:, h * HD:(h + 1) * HD], cos, sin).astype(jnp.bfloat16)
            for b in range(2):
                q_ref[half * 2 + b, h * BLK:(h + 1) * BLK, :HD] = out[b * BLK:(b + 1) * BLK]
    for i in range(BLOCKS):
        q_ref[i, :, HD:] = (lane == doc_ref[shard * BLOCKS + i]).astype(jnp.bfloat16)


def slot_pair(kv_ref, slot, doc_ref, shard):
    lane = lax.broadcasted_iota(jnp.int32, (BLK, HD), 1)
    marks = [
        jnp.where(lane == doc_ref[shard * BLOCKS + b], 0.0, FAR).astype(jnp.bfloat16)
        for b in range(BLOCKS)
    ]
    pieces = [kv_ref[slot, 2 * b * BLK:(2 * b + 1) * BLK, :] for b in range(BLOCKS)]
    keys = jnp.concatenate([jnp.concatenate(pieces, axis=0), jnp.concatenate(marks, axis=0)], axis=1)
    columns = [kv_ref[slot, (2 * b + 1) * BLK:(2 * b + 2) * BLK, :] for b in range(BLOCKS)]
    values = jnp.concatenate(
        [jnp.concatenate(columns, axis=1), jnp.ones((16, ROWS), jnp.bfloat16)], axis=0
    )
    return keys, values


def scores_of(keys, q):
    return lax.dot_general(keys, q, (((1,), (1,)), ((), ())), preferred_element_type=jnp.float32)


def fold_own(q_ref, keys, values, m_ref, acc_ref):
    token = lax.broadcasted_iota(jnp.int32, (BLK, HEADS * BLK), 1) % BLK
    key = lax.broadcasted_iota(jnp.int32, (BLK, HEADS * BLK), 0)
    causal = key <= token
    for i in range(BLOCKS):
        width = (i + 1) * BLK
        scores = scores_of(keys[:width], q_ref[i])
        last = jnp.where(causal, scores[width - BLK:], FAR)
        scores = last if i == 0 else jnp.concatenate([scores[:width - BLK], last], axis=0)
        top = jnp.max(scores, axis=0, keepdims=True)
        weights = jnp.exp2(scores - top).astype(jnp.bfloat16)
        acc_ref[i] = jnp.dot(values[:, :width], weights, preferred_element_type=jnp.float32)
        m_ref[i, 0:1, :] = top


def fold_shard(q_ref, keys, values, m_ref, acc_ref):
    scores = scores_of(keys, q_ref[0])
    for i in range(BLOCKS):
        following = scores_of(keys, q_ref[i + 1]) if i + 1 < BLOCKS else None
        old = m_ref[i, 0:1, :]
        new = jnp.maximum(old, jnp.max(scores, axis=0, keepdims=True))
        weights = jnp.exp2(scores - new).astype(jnp.bfloat16)
        factor = jnp.exp2(old - new)
        product = jnp.dot(values, weights, preferred_element_type=jnp.float32)
        acc_ref[i] = acc_ref[i] * factor + product
        m_ref[i, 0:1, :] = new
        scores = following


def write_context(acc_ref, i, ctx_ref):
    for h in range(HEADS):
        columns = pl.ds(h * BLK, BLK)
        scaled = acc_ref[i, :HD, columns] / acc_ref[i, HD:HD + 1, columns]
        ctx_ref[:, columns] = scaled.T.astype(jnp.bfloat16)


def kernel(
    doc_ref, tok_hbm, gain_ref, wq_hbm, wk_hbm, wv_hbm, freq_ref, wo_hbm, out_ref,
    tok_ref, wkv_ref, wq_ref, wo_ref, normed_ref, cos_ref, sin_ref, q_ref, kv_ref, m_ref, acc_ref,
    ctx_ref, rows_ref, mine_ref, give_ref, take_ref, pass_ref, half_ref, last_ref,
    load_sem, kv_send, kv_recv, give_send, give_recv, pass_send, half_recv, last_recv,
):
    shard = lax.axis_index("seq")
    part = lax.axis_index("tp")
    z, y = shard // 4, shard % 4
    x, c = part // 2, part % 2

    def at_seq(zz, yy):
        return (((zz + 4) % 4) * 4 + (yy + 4) % 4, part)

    def at_tp(xx, cc):
        return (shard, ((xx + 4) % 4) * 2 + cc)

    loads = []
    for n in range(4):
        rows = pl.ds(n * BLK, BLK)
        loads.append(pltpu.make_async_copy(tok_hbm.at[rows, :], tok_ref.at[rows, :], load_sem.at[n]))
    loads.append(pltpu.make_async_copy(wk_hbm, wkv_ref.at[:, :HD], load_sem.at[4]))
    loads.append(pltpu.make_async_copy(wv_hbm, wkv_ref.at[:, HD:], load_sem.at[5]))
    loads.append(pltpu.make_async_copy(wq_hbm, wq_ref, load_sem.at[6]))
    loads.append(pltpu.make_async_copy(wo_hbm, wo_ref, load_sem.at[7]))
    for n in (0, 4, 5, 1, 2, 3):
        loads[n].start()

    barrier = pltpu.get_barrier_semaphore()
    near = [at_seq(z, y + 1), at_seq(z, y - 1), at_seq(z + 1, y), at_seq(z - 1, y)]
    near += [at_tp(x + 1, c), at_tp(x - 1, c), at_tp(x, 1 - c)]
    for device in near:
        pl.semaphore_signal(barrier, inc=1, device_id=device, device_id_type=MESH)
    first_corner = (z == 0) & (y == 3)
    last_corner = (z == 3) & (y == 0)

    @pl.when(first_corner)
    def _():
        pl.semaphore_signal(barrier, inc=1, device_id=(12, part), device_id_type=MESH)

    @pl.when(last_corner)
    def _():
        pl.semaphore_signal(barrier, inc=1, device_id=(3, part), device_id_type=MESH)

    make_tables(doc_ref, freq_ref, cos_ref, sin_ref, shard)
    def slot_of(j, step):
        return j * 4 + (y + step + 4) % 4

    def move(name, source, target, device, piece):
        rows = pl.ds(piece * (2 * ROWS // PIECES), 2 * ROWS // PIECES)
        return pltpu.make_async_remote_copy(
            src_ref=kv_ref.at[source, rows, :],
            dst_ref=kv_ref.at[target, rows, :],
            send_sem=kv_send.at[name * PIECES + piece],
            recv_sem=kv_recv.at[target * PIECES + piece],
            device_id=device,
            device_id_type=MESH,
        )

    up, down = at_seq(z, y + 1), at_seq(z, y - 1)
    onward = at_seq(z + 1, y)
    transfers = {}
    for j in range(3):
        transfers["right", j] = (j * 4, slot_of(j, 0), slot_of(j, 0), up)
        transfers["left", j] = (j * 4 + 1, slot_of(j, 0), slot_of(j, 0), down)
        transfers["pass right", j] = (j * 4 + 2, slot_of(j, -1), slot_of(j, -1), up)
        transfers["pass left", j] = (j * 4 + 3, slot_of(j, 1), slot_of(j, 1), down)
    transfers["onward", 0] = (12, slot_of(0, 0), slot_of(1, 0), onward)
    transfers["onward", 1] = (13, slot_of(1, 0), slot_of(2, 0), onward)
    transfers["beside", 0] = (14, slot_of(0, -1), slot_of(1, -1), onward)
    transfers["corner", 0] = (15, slot_of(0, 0), 12, (12, part))
    sends = {
        ("right", 0): y <= 2, ("left", 0): y == 0, ("pass right", 0): y == 2, ("pass left", 0): y == 3,
        ("right", 1): (z >= 1) & (y == 3), ("left", 1): z >= 1,
        ("pass right", 1): (z >= 1) & (y != 2), ("pass left", 1): (z >= 1) & (y == 0),
        ("right", 2): z >= 2, ("left", 2): (z >= 2) & (y >= 1),
        ("pass left", 2): (z >= 2) & ((y == 1) | (y == 2)),
        ("onward", 0): z <= 2, ("onward", 1): (z >= 1) & (z <= 2), ("beside", 0): (z <= 2) & (y >= 1),
        ("corner", 0): first_corner,
    }
    arrives = {
        (0, -1): y >= 1, (0, 1): y == 3, (0, 2): y >= 2,
        (1, 0): z >= 1, (1, -1): z >= 1, (1, 1): z >= 1, (1, 2): z >= 1,
        (1, -1, 0): (z >= 1) & (y == 0), (1, -1, 1): (z >= 1) & (y >= 1),
        (2, 0): z >= 2, (2, -1): z >= 2, (2, 1): (z >= 2) & (y <= 2), (2, 2): (z >= 2) & (y <= 1),
        (3, 0): last_corner,
    }

    def start(key, piece):
        @pl.when(sends[key])
        def _():
            move(*transfers[key], piece).start()

    def arrive(events):
        for piece in range(PIECES):
            for key, *then in events:
                j, step = key[:2]
                slot = 12 if j == 3 else slot_of(j, step)

                @pl.when(arrives[key])
                def _(slot=slot, then=then):
                    move(0, slot, slot, up, piece).wait_recv()
                    for other in then:
                        start(other, piece)

    own = y
    per = BLK // NORM_ROWS
    for piece in range(PIECES):
        for n in (2 * piece, 2 * piece + 1):
            loads[n].wait()
            if n == 3:
                loads[6].start()
                loads[7].start()
            lax.fori_loop(
                n * per, n * per + per, lambda i, s: (norm_rows(tok_ref, gain_ref, normed_ref, i), s)[1], 0
            )
        if piece == 0:
            loads[4].wait()
            loads[5].wait()
        project_kv(normed_ref, wkv_ref, cos_ref, sin_ref, kv_ref.at[own], piece)
        if piece == 0:
            pl.semaphore_wait(barrier, len(near) + (first_corner | last_corner).astype(jnp.int32))
        for key in (("onward", 0), ("right", 0), ("left", 0), ("corner", 0)):
            start(key, piece)

    loads[6].wait()
    project_q(normed_ref, wq_ref, cos_ref, sin_ref, q_ref, doc_ref, shard)
    fold_own(q_ref, *slot_pair(kv_ref, own, doc_ref, shard), m_ref, acc_ref)

    order = [
        ((0, -1), [
            ((1, 0), ("onward", 1), ("left", 1), ("right", 1)),
            ((0, -1), ("pass right", 0), ("beside", 0)),
            ((0, 1), ("pass left", 0)),
        ]),
        ((1, 0), []),
        ((0, 1), [((3, 0),)]),
        ((3, 0), []),
        ((1, 1), [
            ((2, 0), ("left", 2), ("right", 2)),
            ((1, 1), ("pass left", 1)),
            ((1, -1, 0), ("pass right", 1)),
        ]),
        ((0, 2), [((0, 2),)]),
        ((2, 0), []),
        ((1, -1), [((2, 1), ("pass left", 2)), ((1, -1, 1), ("pass right", 1))]),
        ((2, 1), []),
        ((2, -1), [((2, -1),)]),
        ((1, 2), [((1, 2),)]),
        ((2, 2), [((2, 2),)]),
    ]

    def step(k, carry):
        row, turn, valid = jnp.int32(0), jnp.int32(0), jnp.int32(0)
        for n, (key, events) in enumerate(order):
            if events:
                @pl.when(k == n)
                def _(events=events):
                    arrive(events)
            here = k == n
            row = jnp.where(here, key[0], row)
            turn = jnp.where(here, (y + key[1] + 4) % 4, turn)
            valid = jnp.where(here, arrives[key].astype(jnp.int32), valid)
        corner = row == 3
        slot = jnp.where(corner, 12, row * 4 + turn)
        source = jnp.where(corner, 3, (z - row) * 4 + turn)

        @pl.when(valid == 1)
        def _():
            fold_shard(q_ref, *slot_pair(kv_ref, slot, doc_ref, source), m_ref, acc_ref)

        return carry

    lax.fori_loop(0, len(order), step, 0)
    for key in sends:
        @pl.when(sends[key])
        def _(key=key):
            for piece in range(PIECES):
                move(*transfers[key], piece).wait_send()

    loads[7].wait()
    span = wo_ref.shape[1] // CUTS

    def give(n):
        return pltpu.make_async_remote_copy(
            src_ref=give_ref.at[n], dst_ref=take_ref.at[n], send_sem=give_send.at[n], recv_sem=give_recv.at[n],
            device_id=at_tp(x, 1 - c), device_id_type=MESH,
        )

    def first(n):
        return pltpu.make_async_remote_copy(
            src_ref=pass_ref.at[0, n], dst_ref=half_ref.at[n], send_sem=pass_send.at[n], recv_sem=half_recv.at[n],
            device_id=at_tp(x + (1 if n < CUTS // 2 else -1), c), device_id_type=MESH,
        )

    def final(k, n):
        return pltpu.make_async_remote_copy(
            src_ref=pass_ref.at[k, n], dst_ref=last_ref.at[k - 1, n],
            send_sem=pass_send.at[CUTS * k + n], recv_sem=last_recv.at[CUTS * (k - 1) + n],
            device_id=at_tp(x + 3 - 2 * k, c), device_id_type=MESH,
        )

    targets = [(x + 2) % 4, (x + 1) % 4, (x + 3) % 4, x]
    for k in range(4):
        write_context(acc_ref, targets[k], ctx_ref.at[k])
    theirs = pl.ds(pl.multiple_of((1 - c) * 64, 64), 64)
    ours = pl.ds(pl.multiple_of(c * 64, 64), 64)
    for k in range(4):
        rows_ref[k * 64:(k + 1) * 64, :] = ctx_ref[k, theirs, :]
        rows_ref[(4 + k) * 64:(5 + k) * 64, :] = ctx_ref[k, ours, :]

    def project(n):
        product = jnp.dot(
            rows_ref[...], wo_ref[:, n * span:(n + 1) * span], preferred_element_type=jnp.float32
        )
        for k in range(4):
            give_ref[n, k] = product[k * 64:(k + 1) * 64].astype(jnp.bfloat16)
        give(n).start()
        for k in range(4):
            mine_ref[n, k] = product[(4 + k) * 64:(5 + k) * 64]

    def paired(k, n):
        return mine_ref[n, k] + take_ref[n, k].astype(jnp.float32)

    def send_early(n):
        give(n).wait_recv()
        pass_ref[0, n] = paired(0, n).astype(jnp.bfloat16)
        first(n).start()
        k = 2 if n < CUTS // 2 else 1
        pass_ref[k, n] = paired(k, n).astype(jnp.bfloat16)
        final(k, n).start()

    def send_late(n):
        k = 1 if n < CUTS // 2 else 2
        total = paired(k, n)
        first(n).wait_recv()
        pass_ref[k, n] = (total + half_ref[n].astype(jnp.float32)).astype(jnp.bfloat16)
        final(k, n).start()

    turn = [n // 2 + (n % 2) * (CUTS // 2) for n in range(CUTS)]
    for at in range(CUTS + 1):
        if at < CUTS:
            project(turn[at])
        if at > 0:
            send_early(turn[at - 1])
    for n in turn:
        send_late(n)
    for n in turn:
        k = 2 if n < CUTS // 2 else 1
        total = paired(3, n)
        final(k, n).wait_recv()
        mine_ref[n, 3] = total + last_ref[k - 1, n].astype(jnp.float32)
    for n in turn:
        k = 1 if n < CUTS // 2 else 2
        final(k, n).wait_recv()
        total = mine_ref[n, 3] + last_ref[k - 1, n].astype(jnp.float32)
        out_ref[:, n * span:(n + 1) * span] = total.astype(jnp.bfloat16)
    for n in range(CUTS):
        give(n).wait_send()
        first(n).wait_send()
        final(1, n).wait_send()
        final(2, n).wait_send()


def local(tokens, norm_gain, w_query, w_key, w_value, w_out, doc_ids):
    vmem = pl.BlockSpec(memory_space=pltpu.VMEM)
    smem = pl.BlockSpec(memory_space=pltpu.SMEM)
    hbm = pl.BlockSpec(memory_space=pl.ANY)
    width = tokens.shape[1]
    span = w_out.shape[1] // CUTS
    b16, f32 = jnp.bfloat16, jnp.float32
    dma = pltpu.SemaphoreType.DMA
    return pl.pallas_call(
        kernel,
        out_shape=jax.ShapeDtypeStruct((64, w_out.shape[1]), b16),
        in_specs=[smem, hbm, vmem, hbm, hbm, hbm, vmem, hbm],
        out_specs=vmem,
        scratch_shapes=[
            pltpu.VMEM((ROWS, width), b16),
            pltpu.VMEM((width, 2 * HD), b16),
            pltpu.VMEM((width, HEADS * HD), b16),
            pltpu.VMEM((HEADS * HD, w_out.shape[1]), b16),
            pltpu.VMEM((ROWS, width), b16),
            pltpu.VMEM((ROWS, HD), f32),
            pltpu.VMEM((ROWS, HD), f32),
            pltpu.VMEM((BLOCKS, HEADS * BLK, 2 * HD), b16),
            pltpu.VMEM((13, 2 * ROWS, HD), b16),
            pltpu.VMEM((BLOCKS, 8, HEADS * BLK), f32),
            pltpu.VMEM((BLOCKS, HD + 16, HEADS * BLK), f32),
            pltpu.VMEM((4, BLK, HEADS * HD), b16),
            pltpu.VMEM((8 * 64, HEADS * HD), b16),
            pltpu.VMEM((CUTS, 4, 64, span), f32),
            pltpu.VMEM((CUTS, 4, 64, span), b16),
            pltpu.VMEM((CUTS, 4, 64, span), b16),
            pltpu.VMEM((3, CUTS, 64, span), b16),
            pltpu.VMEM((CUTS, 64, span), b16),
            pltpu.VMEM((2, CUTS, 64, span), b16),
            dma((8,)), dma((16 * PIECES,)), dma((13 * PIECES,)),
            dma((CUTS,)), dma((CUTS,)), dma((3 * CUTS,)), dma((CUTS,)), dma((2 * CUTS,)),
        ],
        compiler_params=pltpu.CompilerParams(
            vmem_limit_bytes=58 * 2**20, collective_id=0, has_side_effects=True
        ),
        cost_estimate=pl.CostEstimate(flops=10**10, bytes_accessed=15 * 2**20, transcendentals=10**7),
    )(doc_ids, tokens, norm_gain[None, :], w_query, w_key, w_value, jnp.asarray(frequencies()), w_out)


def solution(mesh):
    placed = (P("seq", None), P(), P(None, "tp"), P(None, "tp"), P(None, "tp"), P("tp", None), P())
    return jax.shard_map(
        local, mesh=mesh, in_specs=placed, out_specs=P(("seq", "tp"), None), check_vma=False
    )
```

```python
import math

import jax
import jax.numpy as jnp
import numpy as np
from jax import lax
from jax.experimental import pallas as pl
from jax.experimental.pallas import tpu as pltpu
from jax.sharding import PartitionSpec as P

HD = 128
BLK = 128
ROWS = 512
BLOCKS = ROWS // BLK
HEADS = 4
PIECES = 2
CUTS = 8
NORM_ROWS = 32
MESH = pl.DeviceIdType.MESH
FAR = -1e30
rope_base = 500000.0
norm_epsilon = 1e-05
SCALE = HD ** (-0.5) * math.log2(math.e)


def frequencies():
    half = HD // 2
    inverse = np.exp(np.arange(half, dtype=np.float32) * np.float32(-2.0 * math.log(rope_base) / HD))
    return np.concatenate([inverse, inverse])[None, :].astype(np.float32)


def norm_rows(tok_ref, gain_ref, normed_ref, step):
    rows = pl.ds(pl.multiple_of(step * NORM_ROWS, NORM_ROWS), NORM_ROWS)
    width = tok_ref.shape[1]
    squares = jnp.zeros((NORM_ROWS, HD), jnp.float32)
    for at in range(0, width, HD):
        floats = tok_ref[rows, at:at + HD].astype(jnp.float32)
        squares = squares + floats * floats
    mean = jnp.sum(squares, axis=1, keepdims=True) * (1.0 / width)
    factor = lax.rsqrt(mean + norm_epsilon)
    for at in range(0, width, HD):
        floats = tok_ref[rows, at:at + HD].astype(jnp.float32)
        normed_ref[rows, at:at + HD] = (floats * factor * gain_ref[:, at:at + HD]).astype(jnp.bfloat16)


def block_start(doc_ref, block):
    mine = doc_ref[block]

    def count(j, total):
        return total + (doc_ref[j] < mine).astype(jnp.int32)

    return lax.fori_loop(0, doc_ref.shape[0], count, jnp.int32(0), unroll=True) * BLK


def make_tables(doc_ref, freq_ref, cos_ref, sin_ref, shard):
    lane = lax.broadcasted_iota(jnp.int32, (BLK, HD), 1)
    row = lax.broadcasted_iota(jnp.int32, (BLK, HD), 0)

    def one(b, carry):
        block = shard * BLOCKS + b
        offset = row + (block * BLK - block_start(doc_ref, block))
        angle = offset.astype(jnp.float32) * freq_ref[...]
        rows = pl.ds(pl.multiple_of(b * BLK, BLK), BLK)
        cos_ref[rows, :] = jnp.cos(angle)
        sine = jnp.sin(angle)
        sin_ref[rows, :] = jnp.where(lane < HD // 2, -sine, sine)
        return carry

    lax.fori_loop(0, BLOCKS, one, 0)


def rotated(raw, cos, sin):
    return raw * cos + pltpu.roll(raw, HD // 2, 1) * sin


def project_kv(normed_ref, wkv_ref, cos_ref, sin_ref, kv_ref, half):
    rows = pl.ds(half * 256, 256)
    raw = jnp.dot(normed_ref[rows, :], wkv_ref[...], preferred_element_type=jnp.float32)
    keys = rotated(raw[:, :HD], cos_ref[rows, :], sin_ref[rows, :]).astype(jnp.bfloat16)
    for b in range(2):
        at = (half * 2 + b) * 2 * BLK
        kv_ref[at:at + BLK, :] = keys[b * BLK:(b + 1) * BLK]
        kv_ref[at + BLK:at + 2 * BLK, :] = raw[b * BLK:(b + 1) * BLK, HD:].T.astype(jnp.bfloat16)


def project_q(normed_ref, wq_ref, cos_ref, sin_ref, q_ref, doc_ref, shard):
    lane = lax.broadcasted_iota(jnp.int32, (HEADS * BLK, HD), 1)
    for half in range(2):
        rows = pl.ds(half * 256, 256)
        raw = jnp.dot(normed_ref[rows, :], wq_ref[...], preferred_element_type=jnp.float32)
        cos = cos_ref[rows, :] * SCALE
        sin = sin_ref[rows, :] * SCALE
        for h in range(HEADS):
            out = rotated(raw[:, h * HD:(h + 1) * HD], cos, sin).astype(jnp.bfloat16)
            for b in range(2):
                q_ref[half * 2 + b, h * BLK:(h + 1) * BLK, :HD] = out[b * BLK:(b + 1) * BLK]
    for i in range(BLOCKS):
        q_ref[i, :, HD:] = (lane == doc_ref[shard * BLOCKS + i]).astype(jnp.bfloat16)


def slot_pair(kv_ref, slot, doc_ref, shard):
    lane = lax.broadcasted_iota(jnp.int32, (BLK, HD), 1)
    marks = [
        jnp.where(lane == doc_ref[shard * BLOCKS + b], 0.0, FAR).astype(jnp.bfloat16)
        for b in range(BLOCKS)
    ]
    pieces = [kv_ref[slot, 2 * b * BLK:(2 * b + 1) * BLK, :] for b in range(BLOCKS)]
    keys = jnp.concatenate([jnp.concatenate(pieces, axis=0), jnp.concatenate(marks, axis=0)], axis=1)
    columns = [kv_ref[slot, (2 * b + 1) * BLK:(2 * b + 2) * BLK, :] for b in range(BLOCKS)]
    values = jnp.concatenate(
        [jnp.concatenate(columns, axis=1), jnp.ones((16, ROWS), jnp.bfloat16)], axis=0
    )
    return keys, values


def scores_of(keys, q):
    return lax.dot_general(keys, q, (((1,), (1,)), ((), ())), preferred_element_type=jnp.float32)


def fold_own(q_ref, keys, values, m_ref, acc_ref):
    token = lax.broadcasted_iota(jnp.int32, (BLK, HEADS * BLK), 1) % BLK
    key = lax.broadcasted_iota(jnp.int32, (BLK, HEADS * BLK), 0)
    causal = key <= token
    for i in range(BLOCKS):
        width = (i + 1) * BLK
        scores = scores_of(keys[:width], q_ref[i])
        last = jnp.where(causal, scores[width - BLK:], FAR)
        scores = last if i == 0 else jnp.concatenate([scores[:width - BLK], last], axis=0)
        top = jnp.max(scores, axis=0, keepdims=True)
        weights = jnp.exp2(scores - top).astype(jnp.bfloat16)
        acc_ref[i] = jnp.dot(values[:, :width], weights, preferred_element_type=jnp.float32)
        m_ref[i, 0:1, :] = top


def fold_shard(q_ref, keys, values, m_ref, acc_ref):
    scores = scores_of(keys, q_ref[0])
    for i in range(BLOCKS):
        following = scores_of(keys, q_ref[i + 1]) if i + 1 < BLOCKS else None
        old = m_ref[i, 0:1, :]
        new = jnp.maximum(old, jnp.max(scores, axis=0, keepdims=True))
        weights = jnp.exp2(scores - new).astype(jnp.bfloat16)
        factor = jnp.exp2(old - new)
        product = jnp.dot(values, weights, preferred_element_type=jnp.float32)
        acc_ref[i] = acc_ref[i] * factor + product
        m_ref[i, 0:1, :] = new
        scores = following


def write_context(acc_ref, i, ctx_ref):
    for h in range(HEADS):
        columns = pl.ds(h * BLK, BLK)
        scaled = acc_ref[i, :HD, columns] / acc_ref[i, HD:HD + 1, columns]
        ctx_ref[:, columns] = scaled.T.astype(jnp.bfloat16)


def kernel(
    doc_ref, tok_hbm, gain_ref, wq_hbm, wk_hbm, wv_hbm, freq_ref, wo_hbm, out_ref,
    tok_ref, wkv_ref, wq_ref, wo_ref, normed_ref, cos_ref, sin_ref, q_ref, kv_ref, m_ref, acc_ref,
    ctx_ref, rows_ref, mine_ref, give_ref, take_ref, pass_ref, half_ref, last_ref,
    load_sem, kv_send, kv_recv, give_send, give_recv, pass_send, half_recv, last_recv,
):
    shard = lax.axis_index("seq")
    part = lax.axis_index("tp")
    z, y = shard // 4, shard % 4
    x, c = part // 2, part % 2

    def at_seq(zz, yy):
        return (((zz + 4) % 4) * 4 + (yy + 4) % 4, part)

    def at_tp(xx, cc):
        return (shard, ((xx + 4) % 4) * 2 + cc)

    loads = []
    for n in range(4):
        rows = pl.ds(n * BLK, BLK)
        loads.append(pltpu.make_async_copy(tok_hbm.at[rows, :], tok_ref.at[rows, :], load_sem.at[n]))
    loads.append(pltpu.make_async_copy(wk_hbm, wkv_ref.at[:, :HD], load_sem.at[4]))
    loads.append(pltpu.make_async_copy(wv_hbm, wkv_ref.at[:, HD:], load_sem.at[5]))
    loads.append(pltpu.make_async_copy(wq_hbm, wq_ref, load_sem.at[6]))
    loads.append(pltpu.make_async_copy(wo_hbm, wo_ref, load_sem.at[7]))
    for n in (0, 4, 5, 1, 2, 3):
        loads[n].start()

    barrier = pltpu.get_barrier_semaphore()
    near = [at_seq(z, y + 1), at_seq(z, y - 1), at_seq(z + 1, y), at_seq(z - 1, y)]
    near += [at_tp(x + 1, c), at_tp(x - 1, c), at_tp(x, 1 - c)]
    for device in near:
        pl.semaphore_signal(barrier, inc=1, device_id=device, device_id_type=MESH)
    first_corner = (z == 0) & (y == 3)
    last_corner = (z == 3) & (y == 0)

    @pl.when(first_corner)
    def _():
        pl.semaphore_signal(barrier, inc=1, device_id=(12, part), device_id_type=MESH)

    @pl.when(last_corner)
    def _():
        pl.semaphore_signal(barrier, inc=1, device_id=(3, part), device_id_type=MESH)

    make_tables(doc_ref, freq_ref, cos_ref, sin_ref, shard)
    def slot_of(j, step):
        return j * 4 + (y + step + 4) % 4

    def move(name, source, target, device, piece):
        rows = pl.ds(piece * (2 * ROWS // PIECES), 2 * ROWS // PIECES)
        return pltpu.make_async_remote_copy(
            src_ref=kv_ref.at[source, rows, :],
            dst_ref=kv_ref.at[target, rows, :],
            send_sem=kv_send.at[name * PIECES + piece],
            recv_sem=kv_recv.at[target * PIECES + piece],
            device_id=device,
            device_id_type=MESH,
        )

    up, down = at_seq(z, y + 1), at_seq(z, y - 1)
    onward = at_seq(z + 1, y)
    transfers = {}
    for j in range(3):
        transfers["right", j] = (j * 4, slot_of(j, 0), slot_of(j, 0), up)
        transfers["left", j] = (j * 4 + 1, slot_of(j, 0), slot_of(j, 0), down)
        transfers["pass right", j] = (j * 4 + 2, slot_of(j, -1), slot_of(j, -1), up)
        transfers["pass left", j] = (j * 4 + 3, slot_of(j, 1), slot_of(j, 1), down)
    transfers["onward", 0] = (12, slot_of(0, 0), slot_of(1, 0), onward)
    transfers["onward", 1] = (13, slot_of(1, 0), slot_of(2, 0), onward)
    transfers["beside", 0] = (14, slot_of(0, -1), slot_of(1, -1), onward)
    transfers["later", 0] = transfers["beside", 0]
    transfers["corner", 0] = (15, slot_of(0, 0), 12, (12, part))
    sends = {
        ("right", 0): y <= 2, ("left", 0): y == 0, ("pass right", 0): y == 2, ("pass left", 0): y == 3,
        ("right", 1): (z >= 1) & (y == 3), ("left", 1): z >= 1,
        ("pass right", 1): (z >= 1) & (y != 2), ("pass left", 1): (z >= 1) & (y == 0),
        ("right", 2): z >= 2, ("left", 2): (z >= 2) & (y >= 1),
        ("pass left", 2): (z >= 2) & ((y == 1) | (y == 2)),
        ("onward", 0): z <= 2, ("onward", 1): (z >= 1) & (z <= 2), ("beside", 0): (z == 0) & (y >= 1),
        ("later", 0): (z >= 1) & (z <= 2) & (y >= 1),
        ("corner", 0): first_corner,
    }
    arrives = {
        (0, -1): y >= 1, (0, 1): y == 3, (0, 2): y >= 2,
        (1, 0): z >= 1, (1, -1): z >= 1, (1, 1): z >= 1, (1, 2): z >= 1,
        (1, -1, 0): (z >= 1) & (y == 0), (1, -1, 1): (z >= 1) & (y >= 1),
        (2, 0): z >= 2, (2, -1): z >= 2, (2, 1): (z >= 2) & (y <= 2), (2, 2): (z >= 2) & (y <= 1),
        (3, 0): last_corner,
    }

    def start(key, piece):
        @pl.when(sends[key])
        def _():
            move(*transfers[key], piece).start()

    def arrive(events):
        for piece in range(PIECES):
            for key, *then in events:
                j, step = key[:2]
                slot = 12 if j == 3 else slot_of(j, step)

                @pl.when(arrives[key])
                def _(slot=slot, then=then):
                    move(0, slot, slot, up, piece).wait_recv()
                    for other in then:
                        start(other, piece)

    own = y
    per = BLK // NORM_ROWS
    for piece in range(PIECES):
        for n in (2 * piece, 2 * piece + 1):
            loads[n].wait()
            if n == 2:
                loads[6].start()
            if n == 3:
                loads[7].start()
            lax.fori_loop(
                n * per, n * per + per, lambda i, s: (norm_rows(tok_ref, gain_ref, normed_ref, i), s)[1], 0
            )
        if piece == 0:
            loads[4].wait()
            loads[5].wait()
        project_kv(normed_ref, wkv_ref, cos_ref, sin_ref, kv_ref.at[own], piece)
        if piece == 0:
            pl.semaphore_wait(barrier, len(near) + (first_corner | last_corner).astype(jnp.int32))
        for key in (("onward", 0), ("right", 0), ("left", 0), ("corner", 0)):
            start(key, piece)

    loads[6].wait()
    project_q(normed_ref, wq_ref, cos_ref, sin_ref, q_ref, doc_ref, shard)
    fold_own(q_ref, *slot_pair(kv_ref, own, doc_ref, shard), m_ref, acc_ref)

    order = [
        ((0, -1), [
            ((1, 0), ("onward", 1), ("left", 1), ("right", 1)),
            ((0, -1), ("pass right", 0), ("beside", 0)),
            ((0, 1), ("pass left", 0)),
        ]),
        ((1, 0), []),
        ((0, 1), [((3, 0),)]),
        ((3, 0), []),
        ((1, 1), [
            ((2, 0), ("left", 2), ("right", 2)),
            ((1, 1), ("pass left", 1)),
            ((1, -1, 0), ("pass right", 1)),
        ]),
        ((0, 2), [((0, 2),)]),
        ((2, 0), []),
        ((1, -1), [((2, 1), ("pass left", 2)), ((1, -1, 1), ("pass right", 1))]),
        ((2, 1), []),
        ((2, -1), [((2, -1),)]),
        ((1, 2), [((1, 2),)]),
        ((2, 2), [((2, 2),)]),
    ]

    def step(k, carry):
        row, turn, valid = jnp.int32(0), jnp.int32(0), jnp.int32(0)
        for n, (key, events) in enumerate(order):
            if events:
                @pl.when(k == n)
                def _(events=events, n=n):
                    arrive(events)
                    if n == 2:
                        for piece in range(PIECES):
                            start(("later", 0), piece)
            here = k == n
            row = jnp.where(here, key[0], row)
            turn = jnp.where(here, (y + key[1] + 4) % 4, turn)
            valid = jnp.where(here, arrives[key].astype(jnp.int32), valid)
        corner = row == 3
        slot = jnp.where(corner, 12, row * 4 + turn)
        source = jnp.where(corner, 3, (z - row) * 4 + turn)

        @pl.when(valid == 1)
        def _():
            fold_shard(q_ref, *slot_pair(kv_ref, slot, doc_ref, source), m_ref, acc_ref)

        return carry

    lax.fori_loop(0, len(order), step, 0)
    loads[7].wait()
    span = wo_ref.shape[1] // CUTS

    def give(n):
        return pltpu.make_async_remote_copy(
            src_ref=give_ref.at[n], dst_ref=take_ref.at[n], send_sem=give_send.at[n], recv_sem=give_recv.at[n],
            device_id=at_tp(x, 1 - c), device_id_type=MESH,
        )

    def first(n):
        return pltpu.make_async_remote_copy(
            src_ref=pass_ref.at[0, n], dst_ref=half_ref.at[n], send_sem=pass_send.at[n], recv_sem=half_recv.at[n],
            device_id=at_tp(x + (1 if n < CUTS // 2 else -1), c), device_id_type=MESH,
        )

    def final(k, n):
        return pltpu.make_async_remote_copy(
            src_ref=pass_ref.at[k, n], dst_ref=last_ref.at[k - 1, n],
            send_sem=pass_send.at[CUTS * k + n], recv_sem=last_recv.at[CUTS * (k - 1) + n],
            device_id=at_tp(x + 3 - 2 * k, c), device_id_type=MESH,
        )

    targets = [(x + 2) % 4, (x + 1) % 4, (x + 3) % 4, x]
    for k in range(4):
        write_context(acc_ref, targets[k], ctx_ref.at[k])
    theirs = pl.ds(pl.multiple_of((1 - c) * 64, 64), 64)
    ours = pl.ds(pl.multiple_of(c * 64, 64), 64)
    for k in range(4):
        rows_ref[k * 64:(k + 1) * 64, :] = ctx_ref[k, theirs, :]
        rows_ref[(4 + k) * 64:(5 + k) * 64, :] = ctx_ref[k, ours, :]

    def project(n):
        product = jnp.dot(
            rows_ref[...], wo_ref[:, n * span:(n + 1) * span], preferred_element_type=jnp.float32
        )
        for k in range(4):
            give_ref[n, k] = product[k * 64:(k + 1) * 64].astype(jnp.bfloat16)
        give(n).start()
        for k in range(4):
            mine_ref[n, k] = product[(4 + k) * 64:(5 + k) * 64]

    def paired(k, n):
        return mine_ref[n, k] + take_ref[n, k].astype(jnp.float32)

    def send_early(n):
        give(n).wait_recv()
        pass_ref[0, n] = paired(0, n).astype(jnp.bfloat16)
        first(n).start()
        k = 2 if n < CUTS // 2 else 1
        pass_ref[k, n] = paired(k, n).astype(jnp.bfloat16)
        final(k, n).start()

    def send_late(n):
        k = 1 if n < CUTS // 2 else 2
        total = paired(k, n)
        first(n).wait_recv()
        pass_ref[k, n] = (total + half_ref[n].astype(jnp.float32)).astype(jnp.bfloat16)
        final(k, n).start()

    turn = [n // 2 + (n % 2) * (CUTS // 2) for n in range(CUTS)]
    for at in range(CUTS + 1):
        if at < CUTS:
            project(turn[at])
        if at > 0:
            send_early(turn[at - 1])
    for n in turn:
        send_late(n)
    for n in turn:
        k = 2 if n < CUTS // 2 else 1
        total = paired(3, n)
        final(k, n).wait_recv()
        mine_ref[n, 3] = total + last_ref[k - 1, n].astype(jnp.float32)
    for n in turn:
        k = 1 if n < CUTS // 2 else 2
        final(k, n).wait_recv()
        total = mine_ref[n, 3] + last_ref[k - 1, n].astype(jnp.float32)
        out_ref[:, n * span:(n + 1) * span] = total.astype(jnp.bfloat16)
    for key in sends:
        @pl.when(sends[key])
        def _(key=key):
            for piece in range(PIECES):
                move(*transfers[key], piece).wait_send()

    for n in range(CUTS):
        give(n).wait_send()
        first(n).wait_send()
        final(1, n).wait_send()
        final(2, n).wait_send()


def local(tokens, norm_gain, w_query, w_key, w_value, w_out, doc_ids):
    vmem = pl.BlockSpec(memory_space=pltpu.VMEM)
    smem = pl.BlockSpec(memory_space=pltpu.SMEM)
    hbm = pl.BlockSpec(memory_space=pl.ANY)
    width = tokens.shape[1]
    span = w_out.shape[1] // CUTS
    b16, f32 = jnp.bfloat16, jnp.float32
    dma = pltpu.SemaphoreType.DMA
    return pl.pallas_call(
        kernel,
        out_shape=jax.ShapeDtypeStruct((64, w_out.shape[1]), b16),
        in_specs=[smem, hbm, vmem, hbm, hbm, hbm, vmem, hbm],
        out_specs=vmem,
        scratch_shapes=[
            pltpu.VMEM((ROWS, width), b16),
            pltpu.VMEM((width, 2 * HD), b16),
            pltpu.VMEM((width, HEADS * HD), b16),
            pltpu.VMEM((HEADS * HD, w_out.shape[1]), b16),
            pltpu.VMEM((ROWS, width), b16),
            pltpu.VMEM((ROWS, HD), f32),
            pltpu.VMEM((ROWS, HD), f32),
            pltpu.VMEM((BLOCKS, HEADS * BLK, 2 * HD), b16),
            pltpu.VMEM((13, 2 * ROWS, HD), b16),
            pltpu.VMEM((BLOCKS, 8, HEADS * BLK), f32),
            pltpu.VMEM((BLOCKS, HD + 16, HEADS * BLK), f32),
            pltpu.VMEM((4, BLK, HEADS * HD), b16),
            pltpu.VMEM((8 * 64, HEADS * HD), b16),
            pltpu.VMEM((CUTS, 4, 64, span), f32),
            pltpu.VMEM((CUTS, 4, 64, span), b16),
            pltpu.VMEM((CUTS, 4, 64, span), b16),
            pltpu.VMEM((3, CUTS, 64, span), b16),
            pltpu.VMEM((CUTS, 64, span), b16),
            pltpu.VMEM((2, CUTS, 64, span), b16),
            dma((8,)), dma((16 * PIECES,)), dma((13 * PIECES,)),
            dma((CUTS,)), dma((CUTS,)), dma((3 * CUTS,)), dma((CUTS,)), dma((2 * CUTS,)),
        ],
        compiler_params=pltpu.CompilerParams(
            vmem_limit_bytes=58 * 2**20, collective_id=0, has_side_effects=True
        ),
        cost_estimate=pl.CostEstimate(flops=10**10, bytes_accessed=15 * 2**20, transcendentals=10**7),
    )(doc_ids, tokens, norm_gain[None, :], w_query, w_key, w_value, jnp.asarray(frequencies()), w_out)


def solution(mesh):
    placed = (P("seq", None), P(), P(None, "tp"), P(None, "tp"), P(None, "tp"), P("tp", None), P())
    return jax.shard_map(
        local, mesh=mesh, in_specs=placed, out_specs=P(("seq", "tp"), None), check_vma=False
    )
```
